32 devices in a mesh: parts: 2 (over y), tm: 4 (over z), space: 2 (over x), stn: 2 (over core).
Axes of the slice: x: 2, y: 2, z: 4, core: 2. Of those that a mesh axis runs over, the one named last changes fastest.
Arguments:
- fluxes: float32 [64, 4096], P('tm', ('parts', 'space')), parts along dimension 1, may hold values from -6 to 6
- prior_weight: float32 [64, 4096], P('tm', ('parts', 'space')), parts along dimension 1, may hold values from 0.05 to 0.5
- footprint: bfloat16 [256, 64, 4096], P(('tm', 'stn'), None, ('parts', 'space')), parts along dimension 2, may hold values from 1 to 127, as said below
- block_scale: float32 [512, 64], P(('parts', 'tm', 'stn')), parts along dimension 0, as said below
- block_index: int32 [384, 16], P(('parts', 'tm'), 'stn'), parts along dimension 0, may hold values from 0 to 31
- foot_length: int32 [32], P(('parts', 'stn')), parts along dimension 0, may hold values from 1 to 64, as said below
- observed: float32 [384, 16], P(('parts', 'tm'), 'stn'), parts along dimension 0, may hold values from -12 to 12
- obs_weight: float32 [384, 16], P(('parts', 'tm'), 'stn'), parts along dimension 0, may hold values from 0.25 to 2
Outputs:
- weighted_residual: float32 [384, 16], P(('parts', 'tm'), 'stn'), parts along dimension 0
- gradient: float32 [64, 4096], P('tm', ('parts', 'space')), parts along dimension 1
The draws below stay inside these ranges and needn't reach their ends.
There are 2 independent parts, one for each index of `parts`. The reference program is written for one: setup_inputs(seed, part) draws one part's arguments, and reference() takes and returns one part's arrays. A program takes and returns all parts, laid end to end along the dimension named above; each array names one. Nothing has to cross between parts.
Inputs may be any that keep to these rules, and one draw needn't show every extreme that they name: `foot_length`: some station has length 64 and some has length 1. `footprint`: integer codes. `block_scale`: positive.
All inputs are finite; a program needn't handle non-finite values.
Results may differ from the reference program's by a relative error of at most 0.0065.
Values may be sent and summed in bfloat16 or wider, within the bound.
No kernel may reach another device: no remote copies, remote signals or barrier semaphores. Data moves between devices by JAX's collectives and lax.ppermute only.
A program may use at most 64 MiB of HBM per device.

```python
import math
import jax
import jax.numpy as jnp
from jax import lax

SLOT_DEV = 16
STN_DEV = 8
BLK_DEV = 32
LAGS = 64
HOURS_DEV = 48
SLOTS = 64
HOURS = 192
STATIONS = 16
CELLS = 2048
BLOCKS = 256
N_TM = 4
N_STN = 2


def draw_footprint(key, part):
    key = jax.random.fold_in(key, 11)
    codes = jax.random.randint(key, (BLOCKS, LAGS, CELLS), 1, 128, jnp.int32)
    return codes.astype(jnp.float32).astype(jnp.bfloat16)


def draw_block_scale(key, part):
    key = jax.random.fold_in(key, 17)
    factor = 4.0 / (64.0 * (LAGS * CELLS) ** 0.5)
    values = jnp.exp(jax.random.uniform(key, (BLOCKS, LAGS), jnp.float32, jnp.log(0.2), jnp.log(2.0)))
    return values * factor


def draw_foot_length(key, part):
    key = jax.random.fold_in(key, 23)
    first, second = jax.random.split(key)
    lengths = jax.random.randint(first, (STATIONS,), 1, LAGS + 1, jnp.int32)
    order = jax.random.permutation(second, STATIONS)
    station_ids = jnp.arange(STATIONS, dtype=jnp.int32)
    lengths = jnp.where(station_ids == order[0], LAGS, lengths)
    lengths = jnp.where(station_ids == order[1], 1, lengths)
    return lengths.astype(jnp.int32)


def set_ends(result, key, low, top_value):
    shape = result.shape
    place = [jax.random.randint(jax.random.fold_in(key, axis), (), 0, shape[axis]) for axis in range(len(shape))]
    result = result.at[tuple(place)].set(low)
    longest = shape.index(max(shape))
    place[longest] = (place[longest] + 1) % shape[longest]
    return result.at[tuple(place)].set(top_value)


def level_of(key, extent, cuts, least, high):
    def one(position, parts):
        steps = jax.random.uniform(jax.random.fold_in(jax.random.fold_in(key, 6), position), (parts,), jnp.float32, least / len(cuts), high / len(cuts))
        return jnp.repeat(jnp.exp(steps), extent[position] // parts).reshape((-1,) + (1,) * (len(extent) - position - 1))

    loudness = one(*cuts[0])
    for cut in cuts[1:]:
        loudness = loudness * one(*cut)
    return loudness


def centred(rng, dims, scale, bound, cuts=(), kind=jnp.bfloat16):
    gain = level_of(rng, dims, cuts, -0.22, 0.18) if cuts else 1.0
    entries = jax.random.normal(rng, dims, jnp.float32) * scale * gain
    return jnp.minimum(jnp.maximum(entries, -bound), bound).astype(kind)


def setup_inputs(seed: int = 0, part: int = 0) -> dict:
    key_list = jax.random.split(jax.random.key(seed), 9)
    own_keys = jax.random.split(jax.random.fold_in(key_list[8], part), 9)
    fluxes = centred(own_keys[0], (SLOTS, CELLS), 1.0, 6.0, ((0, 4), (1, 2)), jnp.float32)
    prior_weight = jnp.clip(jnp.exp(math.log(0.5) - 2.3025851 * jax.random.uniform(own_keys[1], (SLOTS, CELLS), jnp.float32) ** level_of(own_keys[1], (SLOTS, CELLS), ((0, 4), (1, 2)), -0.2, 0.2)), 0.05, 0.5)
    footprint = draw_footprint(jax.random.fold_in(jax.random.fold_in(key_list[8], part), 71), part)
    block_scale = draw_block_scale(jax.random.fold_in(jax.random.fold_in(key_list[8], part), 71), part)
    block_index = set_ends(jax.random.randint(own_keys[4], (HOURS, STATIONS), 0, BLK_DEV), jax.random.fold_in(own_keys[4], 1), 0, BLK_DEV - 1).astype(jnp.int32)
    foot_length = draw_foot_length(jax.random.fold_in(jax.random.fold_in(key_list[8], part), 71), part)
    observed = centred(own_keys[6], (HOURS, STATIONS), 2.0, 12.0, ((0, 4), (1, 2)), jnp.float32)
    obs_weight = jnp.clip(jnp.exp(math.log(2.0) - 2.0794415 * jax.random.uniform(own_keys[7], (HOURS, STATIONS), jnp.float32) ** level_of(own_keys[7], (HOURS, STATIONS), ((0, 4), (1, 2)), -0.2, 0.2)), 0.25, 2.0)
    return dict(fluxes=fluxes, prior_weight=prior_weight, footprint=footprint, block_scale=block_scale, block_index=block_index, foot_length=foot_length, observed=observed, obs_weight=obs_weight)


def reference(fluxes, prior_weight, footprint, block_scale, block_index, foot_length, observed, obs_weight):
    width = SLOT_DEV + LAGS
    group_blocks = N_STN * BLK_DEV
    padded = jnp.concatenate([jnp.zeros((LAGS, CELLS), jnp.float32), fluxes], 0)
    lag_ids = jnp.arange(LAGS, dtype=jnp.int32)
    in_reach = (lag_ids[None, :] < foot_length[:, None]).astype(jnp.float32)
    hour_ids = jnp.arange(HOURS_DEV, dtype=jnp.int32)
    target = LAGS + hour_ids // 3
    choose = (jnp.arange(width, dtype=jnp.int32)[None, None, :] == target[:, None, None] - lag_ids[None, :, None]).astype(jnp.float32)
    station_group = jnp.arange(STATIONS, dtype=jnp.int32) // STN_DEV
    block_ids = jnp.arange(group_blocks, dtype=jnp.int32)

    def one_shard(step, state):
        grad_pad, residuals = state
        slot_start = (step * SLOT_DEV).astype(jnp.int32)
        hour_start = (step * HOURS_DEV).astype(jnp.int32)
        block_start = (step * group_blocks).astype(jnp.int32)
        window_low = lax.dynamic_slice_in_dim(padded, slot_start, width, 0).astype(jnp.bfloat16)
        table_rows = lax.dynamic_slice_in_dim(footprint, block_start, group_blocks, 0).reshape(group_blocks * LAGS, CELLS)
        scales = lax.dynamic_slice_in_dim(block_scale, block_start, group_blocks, 0)
        products = jnp.dot(table_rows, window_low.T, preferred_element_type=jnp.float32).reshape(group_blocks, LAGS, width)
        block_rows = lax.dynamic_slice_in_dim(block_index, hour_start, HOURS_DEV, 0)
        local_ids = station_group[None, :] * BLK_DEV + block_rows
        picker = (local_ids[:, :, None] == block_ids[None, None, :]).astype(jnp.float32)
        weights_lag = in_reach[None, :, :] * jnp.einsum('hsb,bl->hsl', picker, scales)
        per_row = jnp.einsum('hsb,blj->hslj', picker, products)
        along = jnp.einsum('hslj,hlj->hsl', per_row, choose)
        modeled = jnp.sum(weights_lag * along, axis=2)
        seen = lax.dynamic_slice_in_dim(observed, hour_start, HOURS_DEV, 0)
        weight_rows = lax.dynamic_slice_in_dim(obs_weight, hour_start, HOURS_DEV, 0)
        resid = weight_rows * (modeled - seen)
        spread_rows = jnp.einsum('hsl,hlj->hslj', weights_lag * resid[:, :, None], choose)
        spread = jnp.einsum('hsb,hslj->blj', picker, spread_rows).astype(jnp.bfloat16)
        returned = jnp.dot(spread.reshape(group_blocks * LAGS, width).T, table_rows, preferred_element_type=jnp.float32)
        current = lax.dynamic_slice_in_dim(grad_pad, slot_start, width, 0)
        grad_pad = lax.dynamic_update_slice_in_dim(grad_pad, current + returned, slot_start, 0)
        residuals = lax.dynamic_update_slice_in_dim(residuals, resid, hour_start, 0)
        return grad_pad, residuals

    start_state = (jnp.zeros((LAGS + SLOTS, CELLS), jnp.float32), jnp.zeros((HOURS, STATIONS), jnp.float32))
    grad_pad, residuals = lax.fori_loop(0, N_TM, one_shard, start_state)
    gradient = grad_pad[LAGS:] + prior_weight * fluxes
    return residuals, gradient
```

```python
import functools

import jax
import jax.numpy as jnp
from jax import lax
from jax.experimental import pallas as pl
from jax.experimental.pallas import tpu as pltpu
from jax.sharding import PartitionSpec as P

F32 = jnp.float32
BF16 = jnp.bfloat16
GROUP = 4


def shifted(x, by):
    devices = lax.axis_size("tm")
    pairs = [(i, i + by) for i in range(devices) if 0 <= i + by < devices]
    return lax.ppermute(x, "tm", pairs)


def reach_mask(len_ref, lags, stations):
    shape = (GROUP * lags, GROUP * stations)
    lengths = jnp.concatenate([len_ref[...]] * GROUP, axis=1)
    row = lax.broadcasted_iota(jnp.int32, shape, 0)
    col = lax.broadcasted_iota(jnp.int32, shape, 1)
    same = (row // lags) == (col // stations)
    return jnp.where(same & ((row % lags) < lengths), 1.0, 0.0).astype(BF16)


def lane_scale(scale_ref, groups):
    return jnp.concatenate(
        [scale_ref[pl.ds(i, groups, stride=GROUP), :] for i in range(GROUP)], axis=1
    )


def lag_bits(lags, rows):
    lag = lax.broadcasted_iota(jnp.int32, (rows, GROUP * lags), 1) % lags
    return lag


def two_term_dot(x, mask, contract):
    high = x.astype(BF16)
    low = (x - high.astype(F32)).astype(BF16)
    dims = (((1,), (contract,)), ((), ()))
    return lax.dot_general(high, mask, dims, preferred_element_type=F32) + lax.dot_general(
        low, mask, dims, preferred_element_type=F32
    )


def skew_down(x, lags, slots):
    need = slots + lags
    rows = x.shape[0]
    if rows < need:
        x = jnp.concatenate([jnp.zeros((need - rows, x.shape[1]), x.dtype), x], 0)
    step = lags // 2
    while step >= 8:
        keep = x.shape[0] - step
        bit = (lag_bits(lags, keep) & step) != 0
        x = jnp.where(bit, x[:keep], x[step:])
        step //= 2
    while step >= 1:
        bit = (lag_bits(lags, x.shape[0]) & step) != 0
        x = jnp.where(bit, pltpu.roll(x, step, 0), x)
        step //= 2
    return x[x.shape[0] - slots :]


def skew_up(x, lags, rows):
    slots, lanes = x.shape
    x = jnp.concatenate([jnp.zeros((8, lanes), x.dtype), x], 0)
    step = 1
    while step < 8:
        bit = (lag_bits(lags, x.shape[0]) & step) != 0
        x = jnp.where(bit, pltpu.roll(x, x.shape[0] - step, 0), x)
        step *= 2
    while step < lags:
        gap = jnp.zeros((step, lanes), x.dtype)
        bit = (lag_bits(lags, x.shape[0] + step) & step) != 0
        x = jnp.where(bit, jnp.concatenate([x, gap], 0), jnp.concatenate([gap, x], 0))
        step *= 2
    return x[x.shape[0] - rows :]


def model_kernel(*refs):
    *piece_refs, table_ref, scale_ref, index_ref, len_ref, out_ref = refs
    blocks, lags, cells = table_ref.shape
    slots = piece_refs[0].shape[0]
    hours, stations = index_ref.shape
    per = hours // slots
    groups = blocks // GROUP
    window = jnp.concatenate([r[...].astype(BF16) for r in piece_refs], 0)
    scale = lane_scale(scale_ref, groups)
    mask = reach_mask(len_ref, lags, stations)
    terms = []
    for g in range(groups):
        table = table_ref[g * GROUP : (g + 1) * GROUP].reshape(GROUP * lags, cells)
        products = lax.dot_general(
            window, table, (((1,), (1,)), ((), ())), preferred_element_type=F32
        )
        terms.append(skew_down(products, lags, slots) * scale[g : g + 1])
    sums = two_term_dot(jnp.concatenate(terms, 0), mask, 0)
    lane_block = lax.broadcasted_iota(jnp.int32, (slots, GROUP * stations), 1) // stations
    for k in range(per):
        index = index_ref[pl.ds(k, slots, stride=per), :]
        first = jnp.concatenate([index] * GROUP, axis=1) - lane_block
        picked = jnp.zeros((slots, GROUP * stations), F32)
        for g in range(groups):
            picked = jnp.where(first == g * GROUP, sums[g * slots : (g + 1) * slots], picked)
        total = picked[:, :stations]
        for i in range(1, GROUP):
            total = total + picked[:, i * stations : (i + 1) * stations]
        out_ref[pl.ds(k, slots, stride=per), :] = total


def return_kernel(*refs):
    (mine_ref, other_ref, seen_ref, weight_ref, flux_ref, prior_ref, table_ref, scale_ref,
     index_ref, len_ref, resid_ref, own_ref, *rest) = refs
    *sent_refs, spread_ref = rest
    blocks, lags, cells = table_ref.shape
    slots = flux_ref.shape[0]
    hours, stations = index_ref.shape
    per = hours // slots
    groups = blocks // GROUP
    rows = spread_ref.shape[0]
    scale = lane_scale(scale_ref, groups)
    mask = reach_mask(len_ref, lags, stations)
    lane_block = lax.broadcasted_iota(jnp.int32, (slots, GROUP * stations), 1) // stations
    firsts, resids = [], []
    for k in range(per):
        at = (pl.ds(k, slots, stride=per), slice(None))
        resid = weight_ref[at] * (mine_ref[at] + other_ref[at] - seen_ref[at])
        resid_ref[at] = resid
        resids.append(jnp.concatenate([resid] * GROUP, axis=1))
        firsts.append(jnp.concatenate([index_ref[at]] * GROUP, axis=1) - lane_block)
    placed = []
    for g in range(groups):
        total = jnp.where(firsts[0] == g * GROUP, resids[0], 0.0)
        for k in range(1, per):
            total = total + jnp.where(firsts[k] == g * GROUP, resids[k], 0.0)
        placed.append(total)
    lagged = two_term_dot(jnp.concatenate(placed, 0), mask, 1)
    for g in range(groups):
        term = lagged[g * slots : (g + 1) * slots] * scale[g : g + 1]
        spread = skew_up(term, lags, rows).astype(BF16)
        spread_ref[:, g * GROUP * lags : (g + 1) * GROUP * lags] = spread
    table = table_ref[...].reshape(blocks * lags, cells)
    returned = jnp.dot(spread_ref[...], table, preferred_element_type=F32)
    own_ref[...] = returned[rows - slots :] + 0.5 * prior_ref[...] * flux_ref[...]
    for i, ref in enumerate(sent_refs):
        start = rows - slots * (i + 2)
        ref[...] = returned[start : start + slots].astype(ref.dtype)


VMEM = pl.BlockSpec(memory_space=pltpu.VMEM)


def on_device(
    fluxes, prior_weight, footprint, block_scale, block_index, foot_length, observed, obs_weight
):
    slots, cells = fluxes.shape
    blocks, lags, _ = footprint.shape
    hours, stations = block_index.shape
    far = min(lags // slots, lax.axis_size("tm") - 1)
    rows = slots * (far + 1)
    own = fluxes.astype(BF16)
    pieces = [shifted(own, d) for d in range(far, 0, -1)] + [own]
    lengths = foot_length.reshape(1, stations)
    flops = 2 * blocks * lags * cells * rows
    nbytes = blocks * lags * cells * 2
    cost = pl.CostEstimate(flops=flops, bytes_accessed=nbytes, transcendentals=0)
    params = pltpu.CompilerParams(vmem_limit_bytes=24 * 1024 * 1024)
    mine = pl.pallas_call(
        model_kernel,
        out_shape=jax.ShapeDtypeStruct((hours, stations), F32),
        in_specs=[VMEM] * (len(pieces) + 4),
        out_specs=VMEM,
        compiler_params=params,
        cost_estimate=cost,
    )(*pieces, footprint, block_scale, block_index, lengths)
    other = swapped_sum(mine, "space")
    piece = jax.ShapeDtypeStruct((slots, cells), F32)
    sent = jax.ShapeDtypeStruct((slots, cells), BF16)
    resid, total, *back = pl.pallas_call(
        return_kernel,
        out_shape=[jax.ShapeDtypeStruct((hours, stations), F32), piece] + [sent] * far,
        in_specs=[VMEM] * 10,
        out_specs=[VMEM] * (2 + far),
        scratch_shapes=[pltpu.VMEM((rows, blocks * lags), BF16)],
        compiler_params=params,
        cost_estimate=cost,
    )(mine, other, observed, obs_weight, fluxes, prior_weight, footprint, block_scale, block_index, lengths)
    for d in range(far, 0, -1):
        total = total + shifted(back[d - 1], -d).astype(F32)
    gradient = total + swapped_sum(total, "stn")
    return (resid, gradient)


def swapped_sum(x, axis):
    devices = lax.axis_size(axis)
    total = None
    for by in range(1, devices):
        moved = lax.ppermute(x, axis, [(i, (i + by) % devices) for i in range(devices)])
        total = moved if total is None else total + moved
    return total


def solution(mesh):
    placed = (
        P("tm", ("parts", "space")),
        P("tm", ("parts", "space")),
        P(("tm", "stn"), None, ("parts", "space")),
        P(("parts", "tm", "stn"), None),
        P(("parts", "tm"), "stn"),
        P(("parts", "stn")),
        P(("parts", "tm"), "stn"),
        P(("parts", "tm"), "stn"),
    )
    return jax.shard_map(
        on_device,
        mesh=mesh,
        in_specs=placed,
        out_specs=(P(("parts", "tm"), "stn"), P("tm", ("parts", "space"))),
        check_vma=False,
    )
```

```python
import functools

import jax
import jax.numpy as jnp
from jax import lax
from jax.experimental import pallas as pl
from jax.experimental.pallas import tpu as pltpu
from jax.sharding import PartitionSpec as P

F32 = jnp.float32
BF16 = jnp.bfloat16
GROUP = 4


def shifted(x, by):
    devices = lax.axis_size("tm")
    pairs = [(i, i + by) for i in range(devices) if 0 <= i + by < devices]
    return lax.ppermute(x, "tm", pairs)


def shared(x, near, far):
    devices = lax.axis_size("tm")
    pairs = [
        (t * 2 + core, (t + by) * 2 + core)
        for core, by in ((0, near + 1), (1, near))
        for t in range(devices - by)
        if by <= far
    ]
    return lax.ppermute(x, ("tm", "stn"), pairs)


def reach_mask(len_ref, lags, stations):
    shape = (GROUP * lags, GROUP * stations)
    lengths = jnp.concatenate([len_ref[...]] * GROUP, axis=1)
    row = lax.broadcasted_iota(jnp.int32, shape, 0)
    col = lax.broadcasted_iota(jnp.int32, shape, 1)
    same = (row // lags) == (col // stations)
    return jnp.where(same & ((row % lags) < lengths), 1.0, 0.0).astype(BF16)


def lane_scale(scale_ref, groups):
    return jnp.concatenate(
        [scale_ref[pl.ds(i, groups, stride=GROUP), :] for i in range(GROUP)], axis=1
    )


def lag_bits(lags, rows):
    lag = lax.broadcasted_iota(jnp.int32, (rows, GROUP * lags), 1) % lags
    return lag


def two_term_dot(x, mask, contract):
    high = x.astype(BF16)
    low = (x - high.astype(F32)).astype(BF16)
    dims = (((1,), (contract,)), ((), ()))
    return lax.dot_general(high, mask, dims, preferred_element_type=F32) + lax.dot_general(
        low, mask, dims, preferred_element_type=F32
    )


def skew_down(x, lags, slots):
    need = slots + lags
    rows = x.shape[0]
    if rows < need:
        x = jnp.concatenate([jnp.zeros((need - rows, x.shape[1]), x.dtype), x], 0)
    step = lags // 2
    while step >= 8:
        keep = x.shape[0] - step
        bit = (lag_bits(lags, keep) & step) != 0
        x = jnp.where(bit, x[:keep], x[step:])
        step //= 2
    while step >= 1:
        bit = (lag_bits(lags, x.shape[0]) & step) != 0
        x = jnp.where(bit, pltpu.roll(x, step, 0), x)
        step //= 2
    return x[x.shape[0] - slots :]


def skew_up(x, lags, rows):
    slots, lanes = x.shape
    x = jnp.concatenate([jnp.zeros((8, lanes), x.dtype), x], 0)
    step = 1
    while step < 8:
        bit = (lag_bits(lags, x.shape[0]) & step) != 0
        x = jnp.where(bit, pltpu.roll(x, x.shape[0] - step, 0), x)
        step *= 2
    while step < lags:
        gap = jnp.zeros((step, lanes), x.dtype)
        bit = (lag_bits(lags, x.shape[0] + step) & step) != 0
        x = jnp.where(bit, jnp.concatenate([x, gap], 0), jnp.concatenate([gap, x], 0))
        step *= 2
    return x[x.shape[0] - rows :]


def prepare_kernel(
    scale_hbm, index_hbm, len_hbm, seen_hbm, weight_hbm,
    lane_scale_ref, mask_ref, first_ref, slot_seen_ref, slot_weight_ref,
    scale_ref, index_ref, len_ref, seen_ref, weight_ref, swap_int, swap_float, sems
):
    sources = (scale_hbm, index_hbm, len_hbm, seen_hbm, weight_hbm)
    targets = (scale_ref, index_ref, len_ref, seen_ref, weight_ref)
    copies = [
        pltpu.make_async_copy(source, target, sems.at[i])
        for i, (source, target) in enumerate(zip(sources, targets))
    ]
    for copy in copies:
        copy.start()
    for copy in copies:
        copy.wait()
    groups, width = lane_scale_ref.shape
    stations = index_ref.shape[0]
    per, slots, _ = first_ref.shape
    lane_scale_ref[...] = lane_scale(scale_ref, groups)
    mask_ref[...] = reach_mask(len_ref, width // GROUP, stations)
    lane_block = lax.broadcasted_iota(jnp.int32, (slots, GROUP * stations), 1) // stations
    swap_int[...] = index_ref[...].T
    for k in range(per):
        index = swap_int[pl.ds(k, slots, stride=per), :]
        first_ref[k] = jnp.concatenate([index] * GROUP, axis=1) - lane_block
    for source, target in ((seen_ref, slot_seen_ref), (weight_ref, slot_weight_ref)):
        swap_float[...] = source[...].T
        for k in range(per):
            target[k] = swap_float[pl.ds(k, slots, stride=per), :]


def model_kernel(far, *refs):
    *moved_refs, own_ref, table_ref, scale_ref, mask_ref, first_ref, out_ref = refs
    blocks, lags, cells = table_ref.shape
    per, slots, stations = out_ref.shape
    groups = blocks // GROUP
    core = lax.axis_index("stn")
    got, swapped = moved_refs[: len(moved_refs) // 2], moved_refs[len(moved_refs) // 2 :]
    pieces = [own_ref[...]]
    for mine, other in zip(got, swapped):
        pieces.append(jnp.where(core == 1, mine[...], other[...]))
        pieces.append(jnp.where(core == 0, mine[...], other[...]))
    pieces = pieces[: far + 1][::-1]
    window = jnp.concatenate([p.astype(BF16) for p in pieces], 0)
    scale = scale_ref[...]
    mask = mask_ref[...]
    terms = []
    for g in range(groups):
        table = table_ref[g * GROUP : (g + 1) * GROUP].reshape(GROUP * lags, cells)
        products = lax.dot_general(
            window, table, (((1,), (1,)), ((), ())), preferred_element_type=F32
        )
        terms.append(skew_down(products, lags, slots) * scale[g : g + 1])
    sums = two_term_dot(jnp.concatenate(terms, 0), mask, 0)
    for k in range(per):
        first = first_ref[k]
        picked = jnp.zeros((slots, GROUP * stations), F32)
        for g in range(groups):
            picked = jnp.where(first == g * GROUP, sums[g * slots : (g + 1) * slots], picked)
        total = picked[:, :stations]
        for i in range(1, GROUP):
            total = total + picked[:, i * stations : (i + 1) * stations]
        out_ref[k] = total


def return_kernel(*refs):
    (mine_ref, other_ref, seen_ref, weight_ref, flux_ref, prior_ref, table_ref, scale_ref,
     mask_ref, first_ref, resid_ref, own_ref, *rest) = refs
    *sent_refs, spread_ref, swap_float = rest
    blocks, lags, cells = table_ref.shape
    per, slots, stations = mine_ref.shape
    groups = blocks // GROUP
    rows = spread_ref.shape[0]
    scale = scale_ref[...]
    mask = mask_ref[...]
    firsts, resids = [], []
    for k in range(per):
        resid = weight_ref[k] * (mine_ref[k] + other_ref[k] - seen_ref[k])
        swap_float[pl.ds(k, slots, stride=per), :] = resid
        resids.append(jnp.concatenate([resid] * GROUP, axis=1))
        firsts.append(first_ref[k])
    placed = []
    for g in range(groups):
        total = jnp.where(firsts[0] == g * GROUP, resids[0], 0.0)
        for k in range(1, per):
            total = total + jnp.where(firsts[k] == g * GROUP, resids[k], 0.0)
        placed.append(total)
    lagged = two_term_dot(jnp.concatenate(placed, 0), mask, 1)
    for g in range(groups):
        term = lagged[g * slots : (g + 1) * slots] * scale[g : g + 1]
        spread = skew_up(term, lags, rows).astype(BF16)
        spread_ref[:, g * GROUP * lags : (g + 1) * GROUP * lags] = spread
    table = table_ref[...].reshape(blocks * lags, cells)
    returned = jnp.dot(spread_ref[...], table, preferred_element_type=F32)
    resid_ref[...] = swap_float[...].T
    own_ref[...] = returned[rows - slots :] + 0.5 * prior_ref[...] * flux_ref[...]
    for i, ref in enumerate(sent_refs):
        start = rows - slots * (i + 2)
        ref[...] = returned[start : start + slots].astype(ref.dtype)


PARAMS = pltpu.CompilerParams(vmem_limit_bytes=12 * 1024 * 1024)
VMEM = pl.BlockSpec(memory_space=pltpu.VMEM)


def on_device(
    fluxes, prior_weight, footprint, block_scale, block_index, foot_length, observed, obs_weight
):
    slots, cells = fluxes.shape
    blocks, lags, _ = footprint.shape
    hours, stations = block_index.shape
    far = min(lags // slots, lax.axis_size("tm") - 1)
    rows = slots * (far + 1)
    own = fluxes
    got = [shared(own, d, far) for d in range(1, far + 1, 2)]
    per = hours // slots
    groups = blocks // GROUP
    by_hour = jax.ShapeDtypeStruct((per, slots, stations), F32)
    scale, mask, first, seen, weight = pl.pallas_call(
        prepare_kernel,
        out_shape=[
            jax.ShapeDtypeStruct((groups, GROUP * lags), F32),
            jax.ShapeDtypeStruct((GROUP * lags, GROUP * stations), BF16),
            jax.ShapeDtypeStruct((per, slots, GROUP * stations), jnp.int32),
            by_hour,
            by_hour,
        ],
        in_specs=[pl.BlockSpec(memory_space=pltpu.HBM)] * 5,
        out_specs=[VMEM] * 5,
        scratch_shapes=[
            pltpu.VMEM((blocks, lags), F32),
            pltpu.VMEM((stations, hours), jnp.int32),
            pltpu.VMEM((1, stations), jnp.int32),
            pltpu.VMEM((stations, hours), F32),
            pltpu.VMEM((stations, hours), F32),
            pltpu.VMEM((hours, stations), jnp.int32),
            pltpu.VMEM((hours, stations), F32),
            pltpu.SemaphoreType.DMA((5,)),
        ],
        compiler_params=PARAMS,
        cost_estimate=pl.CostEstimate(flops=2 * 10**10, bytes_accessed=10**5, transcendentals=0),
    )(*[pltpu.with_memory_space_constraint(x, pltpu.HBM) for x in (block_scale, block_index.T, foot_length.reshape(1, stations), observed.T, obs_weight.T)])
    got, scale, mask, first, seen, weight = lax.optimization_barrier(
        (got, scale, mask, first, seen, weight)
    )
    both = swapped_sum(jnp.concatenate(got, 0), "stn")
    pieces = got + [both[i * slots : (i + 1) * slots] for i in range(len(got))] + [own]
    flops = 2 * blocks * lags * cells * rows
    nbytes = blocks * lags * cells * 2
    cost = pl.CostEstimate(flops=flops, bytes_accessed=nbytes, transcendentals=0)
    mine = pl.pallas_call(
        functools.partial(model_kernel, far),
        out_shape=by_hour,
        in_specs=[VMEM] * (len(pieces) + 4),
        out_specs=VMEM,
        compiler_params=PARAMS,
        cost_estimate=cost,
    )(*pieces, footprint, scale, mask, first)
    other = swapped_sum(mine, "space")
    piece = jax.ShapeDtypeStruct((slots, cells), F32)
    sent = jax.ShapeDtypeStruct((slots, cells), BF16)
    resid, total, *back = pl.pallas_call(
        return_kernel,
        out_shape=[jax.ShapeDtypeStruct((stations, hours), F32), piece] + [sent] * far,
        in_specs=[VMEM] * 10,
        out_specs=[VMEM] * (2 + far),
        scratch_shapes=[pltpu.VMEM((rows, blocks * lags), BF16), pltpu.VMEM((hours, stations), F32)],
        compiler_params=PARAMS,
        cost_estimate=cost,
    )(mine, other, seen, weight, fluxes, prior_weight, footprint, scale, mask, first)
    for d in range(far, 0, -1):
        total = total + shifted(back[d - 1], -d).astype(F32)
    gradient = total + swapped_sum(total, "stn")
    return (resid.T, gradient)


def swapped_sum(x, axis):
    devices = lax.axis_size(axis)
    total = None
    for by in range(1, devices):
        moved = lax.ppermute(x, axis, [(i, (i + by) % devices) for i in range(devices)])
        total = moved if total is None else total + moved
    return total


def solution(mesh):
    placed = (
        P("tm", ("parts", "space")),
        P("tm", ("parts", "space")),
        P(("tm", "stn"), None, ("parts", "space")),
        P(("parts", "tm", "stn"), None),
        P(("parts", "tm"), "stn"),
        P(("parts", "stn")),
        P(("parts", "tm"), "stn"),
        P(("parts", "tm"), "stn"),
    )
    return jax.shard_map(
        on_device,
        mesh=mesh,
        in_specs=placed,
        out_specs=(P(("parts", "tm"), "stn"), P("tm", ("parts", "space"))),
        check_vma=False,
    )
```

```python
import functools

import jax
import jax.numpy as jnp
from jax import lax
from jax.experimental import pallas as pl
from jax.experimental.pallas import tpu as pltpu
from jax.sharding import PartitionSpec as P

F32 = jnp.float32
BF16 = jnp.bfloat16
GROUP = 4


def rolled(x, by):
    devices = lax.axis_size("tm")
    return lax.ppermute(x, "tm", [(t, (t + by) % devices) for t in range(devices)])


def shared(x, near):
    devices = lax.axis_size("tm")
    pairs = [
        (t * 2 + core, (t + near + 1 - core) % devices * 2 + core)
        for t in range(devices)
        for core in (0, 1)
    ]
    return lax.ppermute(x, ("tm", "stn"), pairs)


def reach_mask(len_ref, lags, stations):
    shape = (GROUP * lags, GROUP * stations)
    lengths = jnp.concatenate([len_ref[...]] * GROUP, axis=1)
    row = lax.broadcasted_iota(jnp.int32, shape, 0)
    col = lax.broadcasted_iota(jnp.int32, shape, 1)
    same = (row // lags) == (col // stations)
    return jnp.where(same & ((row % lags) < lengths), 1.0, 0.0).astype(BF16)


def lane_scale(scale_ref, groups):
    return jnp.concatenate(
        [scale_ref[pl.ds(i, groups, stride=GROUP), :] for i in range(GROUP)], axis=1
    )


def lag_bits(lags, rows):
    lag = lax.broadcasted_iota(jnp.int32, (rows, GROUP * lags), 1) % lags
    return lag


def two_term_dot(x, mask, contract):
    high = x.astype(BF16)
    low = (x - high.astype(F32)).astype(BF16)
    dims = (((1,), (contract,)), ((), ()))
    return lax.dot_general(high, mask, dims, preferred_element_type=F32) + lax.dot_general(
        low, mask, dims, preferred_element_type=F32
    )


def skew_down(x, lags, slots):
    need = slots + lags
    rows = x.shape[0]
    if rows < need:
        x = jnp.concatenate([jnp.zeros((need - rows, x.shape[1]), x.dtype), x], 0)
    step = lags // 2
    while step >= 8:
        keep = x.shape[0] - step
        bit = (lag_bits(lags, keep) & step) != 0
        x = jnp.where(bit, x[:keep], x[step:])
        step //= 2
    while step >= 1:
        bit = (lag_bits(lags, x.shape[0]) & step) != 0
        x = jnp.where(bit, pltpu.roll(x, step, 0), x)
        step //= 2
    return x[x.shape[0] - slots :]


def skew_up(x, lags, rows):
    slots, lanes = x.shape
    x = jnp.concatenate([jnp.zeros((8, lanes), x.dtype), x], 0)
    step = 1
    while step < 8:
        bit = (lag_bits(lags, x.shape[0]) & step) != 0
        x = jnp.where(bit, pltpu.roll(x, x.shape[0] - step, 0), x)
        step *= 2
    while step < lags:
        gap = jnp.zeros((step, lanes), x.dtype)
        bit = (lag_bits(lags, x.shape[0] + step) & step) != 0
        x = jnp.where(bit, jnp.concatenate([x, gap], 0), jnp.concatenate([gap, x], 0))
        step *= 2
    return x[x.shape[0] - rows :]


def round_kernel(flux_hbm, out_ref, flux_ref, sem):
    copy = pltpu.make_async_copy(flux_hbm, flux_ref, sem)
    copy.start()
    copy.wait()
    out_ref[...] = flux_ref[...].astype(out_ref.dtype)


def model_kernel(far, *refs):
    moved_refs = refs[: far]
    (own_ref, table_ref, block_scale_ref, index_ref, len_ref, seen_ref, weight_ref,
     out_ref, scale_ref, mask_ref, first_ref, slot_seen_ref, slot_weight_ref,
     swap_int, swap_float) = refs[far:]
    blocks, lags, cells = table_ref.shape
    per, slots, stations = out_ref.shape
    groups = blocks // GROUP
    core, shard = lax.axis_index("stn"), lax.axis_index("tm")
    pieces = [own_ref[...]]
    for near in range(1, far + 1, 2):
        if near == far:
            both = [moved_refs[near - 1][...]]
        else:
            mine, other = moved_refs[near - 1][...], moved_refs[near][...]
            both = [jnp.where(core == 1, mine, other), jnp.where(core == 0, mine, other)]
        for distance, piece in enumerate(both, near):
            pieces.append(jnp.where(shard >= distance, piece, jnp.zeros_like(piece)))
    window = jnp.concatenate(pieces[::-1], 0)
    scale = lane_scale(block_scale_ref, groups)
    scale_ref[...] = scale
    mask = reach_mask(len_ref, lags, stations)
    mask_ref[...] = mask
    lane_block = lax.broadcasted_iota(jnp.int32, (slots, GROUP * stations), 1) // stations
    swap_int[...] = index_ref[...].T
    for k in range(per):
        index = swap_int[pl.ds(k, slots, stride=per), :]
        first_ref[k] = jnp.concatenate([index] * GROUP, axis=1) - lane_block
    for i, (source, target) in enumerate(((seen_ref, slot_seen_ref), (weight_ref, slot_weight_ref))):
        swap_float[i] = source[...].T
        for k in range(per):
            target[k] = swap_float[i, pl.ds(k, slots, stride=per), :]
    terms = []
    for g in range(groups):
        table = table_ref[g * GROUP : (g + 1) * GROUP].reshape(GROUP * lags, cells)
        products = lax.dot_general(
            window, table, (((1,), (1,)), ((), ())), preferred_element_type=F32
        )
        terms.append(skew_down(products, lags, slots) * scale[g : g + 1])
    sums = two_term_dot(jnp.concatenate(terms, 0), mask, 0)
    for k in range(per):
        first = first_ref[k]
        picked = jnp.zeros((slots, GROUP * stations), F32)
        for g in range(groups):
            picked = jnp.where(first == g * GROUP, sums[g * slots : (g + 1) * slots], picked)
        total = picked[:, :stations]
        for i in range(1, GROUP):
            total = total + picked[:, i * stations : (i + 1) * stations]
        out_ref[k] = total


def return_kernel(*refs):
    (mine_ref, other_ref, seen_ref, weight_ref, flux_ref, prior_ref, table_ref, scale_ref,
     mask_ref, first_ref, resid_ref, own_ref, *rest) = refs
    *sent_refs, spread_ref = rest
    blocks, lags, cells = table_ref.shape
    per, slots, stations = mine_ref.shape
    groups = blocks // GROUP
    rows = spread_ref.shape[0]
    shard = lax.axis_index("tm")
    scale = scale_ref[...]
    mask = mask_ref[...]
    firsts, resids = [], []
    for k in range(per):
        resid = weight_ref[k] * (mine_ref[k] + other_ref[k] - seen_ref[k])
        resid_ref[k] = resid
        resids.append(jnp.concatenate([resid] * GROUP, axis=1))
        firsts.append(first_ref[k])
    placed = []
    for g in range(groups):
        total = jnp.where(firsts[0] == g * GROUP, resids[0], 0.0)
        for k in range(1, per):
            total = total + jnp.where(firsts[k] == g * GROUP, resids[k], 0.0)
        placed.append(total)
    lagged = two_term_dot(jnp.concatenate(placed, 0), mask, 1)
    for g in range(groups):
        term = lagged[g * slots : (g + 1) * slots] * scale[g : g + 1]
        spread = skew_up(term, lags, rows).astype(BF16)
        spread_ref[:, g * GROUP * lags : (g + 1) * GROUP * lags] = spread
    table = table_ref[...].reshape(blocks * lags, cells)
    returned = jnp.dot(spread_ref[...], table, preferred_element_type=F32)
    own_ref[...] = returned[rows - slots :] + 0.5 * prior_ref[...] * flux_ref[...]
    for i, ref in enumerate(sent_refs):
        start = rows - slots * (i + 2)
        piece = returned[start : start + slots].astype(ref.dtype)
        ref[...] = jnp.where(shard > i, piece, jnp.zeros_like(piece))


def order_kernel(slot_resid_ref, resid_ref, swap_float):
    per, slots, _ = slot_resid_ref.shape
    for k in range(per):
        swap_float[pl.ds(k, slots, stride=per), :] = slot_resid_ref[k]
    resid_ref[...] = swap_float[...].T


PARAMS = pltpu.CompilerParams(vmem_limit_bytes=12 * 1024 * 1024)
VMEM = pl.BlockSpec(memory_space=pltpu.VMEM)


def on_device(
    fluxes, prior_weight, footprint, block_scale, block_index, foot_length, observed, obs_weight
):
    slots, cells = fluxes.shape
    blocks, lags, _ = footprint.shape
    hours, stations = block_index.shape
    far = min(lags // slots, lax.axis_size("tm") - 1)
    rows = slots * (far + 1)
    own = pl.pallas_call(
        round_kernel,
        out_shape=jax.ShapeDtypeStruct((slots, cells), BF16),
        in_specs=[pl.BlockSpec(memory_space=pltpu.HBM)],
        out_specs=VMEM,
        scratch_shapes=[pltpu.VMEM((slots, cells), F32), pltpu.SemaphoreType.DMA],
        compiler_params=pltpu.CompilerParams(vmem_limit_bytes=2 * 1024 * 1024),
        cost_estimate=pl.CostEstimate(flops=2 * 10**10, bytes_accessed=10**5, transcendentals=0),
    )(pltpu.with_memory_space_constraint(fluxes, pltpu.HBM))
    moved = []
    for near in range(1, far + 1, 2):
        if near == far:
            moved.append(rolled(own, near))
        else:
            got = shared(own, near)
            moved += [got, swapped_sum(got, "stn")]
    per = hours // slots
    groups = blocks // GROUP
    by_hour = jax.ShapeDtypeStruct((per, slots, stations), F32)
    flops = 2 * blocks * lags * cells * rows
    nbytes = blocks * lags * cells * 2
    cost = pl.CostEstimate(flops=flops, bytes_accessed=nbytes, transcendentals=0)
    mine, scale, mask, first, seen, weight = pl.pallas_call(
        functools.partial(model_kernel, far),
        out_shape=[
            by_hour,
            jax.ShapeDtypeStruct((groups, GROUP * lags), F32),
            jax.ShapeDtypeStruct((GROUP * lags, GROUP * stations), BF16),
            jax.ShapeDtypeStruct((per, slots, GROUP * stations), jnp.int32),
            by_hour,
            by_hour,
        ],
        in_specs=[VMEM] * (far + 7),
        out_specs=[VMEM] * 6,
        scratch_shapes=[pltpu.VMEM((hours, stations), jnp.int32), pltpu.VMEM((2, hours, stations), F32)],
        compiler_params=PARAMS,
        cost_estimate=cost,
    )(*moved, own, footprint, block_scale, block_index.T, foot_length.reshape(1, stations), observed.T, obs_weight.T)
    other = swapped_sum(mine, "space")
    piece = jax.ShapeDtypeStruct((slots, cells), F32)
    sent = jax.ShapeDtypeStruct((slots, cells), BF16)
    resid, total, *back = pl.pallas_call(
        return_kernel,
        out_shape=[by_hour, piece] + [sent] * far,
        in_specs=[VMEM] * 10,
        out_specs=[VMEM] * (2 + far),
        scratch_shapes=[pltpu.VMEM((rows, blocks * lags), BF16)],
        compiler_params=PARAMS,
        cost_estimate=cost,
    )(mine, other, seen, weight, fluxes, prior_weight, footprint, scale, mask, first)
    for d in range(far, 0, -1):
        total = total + rolled(back[d - 1], -d).astype(F32)
    resid = pl.pallas_call(
        order_kernel,
        out_shape=jax.ShapeDtypeStruct((stations, hours), F32),
        in_specs=[VMEM],
        out_specs=VMEM,
        scratch_shapes=[pltpu.VMEM((hours, stations), F32)],
        compiler_params=pltpu.CompilerParams(vmem_limit_bytes=2 * 1024 * 1024),
        cost_estimate=pl.CostEstimate(flops=10**6, bytes_accessed=10**4, transcendentals=0),
    )(resid)
    gradient = total + swapped_sum(total, "stn")
    return (resid.T, gradient)


def swapped_sum(x, axis):
    devices = lax.axis_size(axis)
    total = None
    for by in range(1, devices):
        moved = lax.ppermute(x, axis, [(i, (i + by) % devices) for i in range(devices)])
        total = moved if total is None else total + moved
    return total


def solution(mesh):
    placed = (
        P("tm", ("parts", "space")),
        P("tm", ("parts", "space")),
        P(("tm", "stn"), None, ("parts", "space")),
        P(("parts", "tm", "stn"), None),
        P(("parts", "tm"), "stn"),
        P(("parts", "stn")),
        P(("parts", "tm"), "stn"),
        P(("parts", "tm"), "stn"),
    )
    return jax.shard_map(
        on_device,
        mesh=mesh,
        in_specs=placed,
        out_specs=(P(("parts", "tm"), "stn"), P("tm", ("parts", "space"))),
        check_vma=False,
    )
```

```python
import functools

import jax
import jax.numpy as jnp
from jax import lax
from jax.experimental import pallas as pl
from jax.experimental.pallas import tpu as pltpu
from jax.sharding import PartitionSpec as P

F32 = jnp.float32
BF16 = jnp.bfloat16
GROUP = 4


def rolled(x, by):
    devices = lax.axis_size("tm")
    return lax.ppermute(x, "tm", [(t, (t + by) % devices) for t in range(devices)])


def shared(x, near, sign=1):
    devices = lax.axis_size("tm")
    pairs = [
        (t * 2 + core, (t + sign * (near + 1 - core)) % devices * 2 + core)
        for t in range(devices)
        for core in (0, 1)
    ]
    return lax.ppermute(x, ("tm", "stn"), pairs)


def reach_mask(len_ref, lags, stations):
    shape = (GROUP * lags, GROUP * stations)
    lengths = jnp.concatenate([len_ref[...]] * GROUP, axis=1)
    row = lax.broadcasted_iota(jnp.int32, shape, 0)
    col = lax.broadcasted_iota(jnp.int32, shape, 1)
    same = (row // lags) == (col // stations)
    return jnp.where(same & ((row % lags) < lengths), 1.0, 0.0).astype(BF16)


def lane_scale(scale_ref, groups):
    return jnp.concatenate(
        [scale_ref[pl.ds(i, groups, stride=GROUP), :] for i in range(GROUP)], axis=1
    )


def lag_bits(lags, rows):
    lag = lax.broadcasted_iota(jnp.int32, (rows, GROUP * lags), 1) % lags
    return lag


def two_term_dot(x, mask, contract):
    high = x.astype(BF16)
    low = (x - high.astype(F32)).astype(BF16)
    dims = (((1,), (contract,)), ((), ()))
    return lax.dot_general(high, mask, dims, preferred_element_type=F32) + lax.dot_general(
        low, mask, dims, preferred_element_type=F32
    )


def skew_down(x, lags, slots):
    need = slots + lags
    rows = x.shape[0]
    if rows < need:
        x = jnp.concatenate([jnp.zeros((need - rows, x.shape[1]), x.dtype), x], 0)
    step = lags // 2
    while step >= 8:
        keep = x.shape[0] - step
        bit = (lag_bits(lags, keep) & step) != 0
        x = jnp.where(bit, x[:keep], x[step:])
        step //= 2
    while step >= 1:
        bit = (lag_bits(lags, x.shape[0]) & step) != 0
        x = jnp.where(bit, pltpu.roll(x, step, 0), x)
        step //= 2
    return x[x.shape[0] - slots :]


def skew_up(x, lags, rows):
    slots, lanes = x.shape
    x = jnp.concatenate([jnp.zeros((8, lanes), x.dtype), x], 0)
    step = 1
    while step < 8:
        bit = (lag_bits(lags, x.shape[0]) & step) != 0
        x = jnp.where(bit, pltpu.roll(x, x.shape[0] - step, 0), x)
        step *= 2
    while step < lags:
        gap = jnp.zeros((step, lanes), x.dtype)
        bit = (lag_bits(lags, x.shape[0] + step) & step) != 0
        x = jnp.where(bit, jnp.concatenate([x, gap], 0), jnp.concatenate([gap, x], 0))
        step *= 2
    return x[x.shape[0] - rows :]


def round_kernel(flux_hbm, out_ref, flux_ref, sem):
    copy = pltpu.make_async_copy(flux_hbm, flux_ref, sem)
    copy.start()
    copy.wait()
    out_ref[...] = flux_ref[...].astype(out_ref.dtype)


def model_kernel(far, *refs):
    moved_refs = refs[: far]
    (own_ref, table_ref, block_scale_ref, index_ref, len_ref, seen_ref, weight_ref,
     out_ref, scale_ref, mask_ref, first_ref, slot_seen_ref, slot_weight_ref,
     swap_int, swap_float) = refs[far:]
    blocks, lags, cells = table_ref.shape
    per, slots, stations = out_ref.shape
    groups = blocks // GROUP
    core, shard = lax.axis_index("stn"), lax.axis_index("tm")
    pieces = [own_ref[...]]
    for near in range(1, far + 1, 2):
        if near == far:
            both = [moved_refs[near - 1][...]]
        else:
            mine, other = moved_refs[near - 1][...], moved_refs[near][...]
            both = [jnp.where(core == 1, mine, other), jnp.where(core == 0, mine, other)]
        for distance, piece in enumerate(both, near):
            pieces.append(jnp.where(shard >= distance, piece, jnp.zeros_like(piece)))
    window = jnp.concatenate(pieces[::-1], 0)
    scale = lane_scale(block_scale_ref, groups)
    scale_ref[...] = scale
    mask = reach_mask(len_ref, lags, stations)
    mask_ref[...] = mask
    lane_block = lax.broadcasted_iota(jnp.int32, (slots, GROUP * stations), 1) // stations
    swap_int[...] = index_ref[...].T
    for k in range(per):
        index = swap_int[pl.ds(k, slots, stride=per), :]
        first_ref[k] = jnp.concatenate([index] * GROUP, axis=1) - lane_block
    for i, (source, target) in enumerate(((seen_ref, slot_seen_ref), (weight_ref, slot_weight_ref))):
        swap_float[i] = source[...].T
        for k in range(per):
            target[k] = swap_float[i, pl.ds(k, slots, stride=per), :]
    terms = []
    for g in range(groups):
        table = table_ref[g * GROUP : (g + 1) * GROUP].reshape(GROUP * lags, cells)
        products = lax.dot_general(
            table, window, (((1,), (1,)), ((), ())), preferred_element_type=F32
        ).T
        terms.append(skew_down(products, lags, slots) * scale[g : g + 1])
    sums = two_term_dot(jnp.concatenate(terms, 0), mask, 0)
    for k in range(per):
        first = first_ref[k]
        picked = jnp.zeros((slots, GROUP * stations), F32)
        for g in range(groups):
            picked = jnp.where(first == g * GROUP, sums[g * slots : (g + 1) * slots], picked)
        total = picked[:, :stations]
        for i in range(1, GROUP):
            total = total + picked[:, i * stations : (i + 1) * stations]
        out_ref[k] = total


def return_kernel(*refs):
    (mine_ref, other_ref, seen_ref, weight_ref, flux_ref, prior_ref, table_ref, scale_ref,
     mask_ref, first_ref, resid_ref, own_ref, *rest) = refs
    *sent_refs, spread_ref = rest
    blocks, lags, cells = table_ref.shape
    per, slots, stations = mine_ref.shape
    groups = blocks // GROUP
    rows = spread_ref.shape[0]
    shard = lax.axis_index("tm")
    scale = scale_ref[...]
    mask = mask_ref[...]
    firsts, resids = [], []
    for k in range(per):
        resid = weight_ref[k] * (mine_ref[k] + other_ref[k] - seen_ref[k])
        resid_ref[k] = resid
        resids.append(jnp.concatenate([resid] * GROUP, axis=1))
        firsts.append(first_ref[k])
    placed = []
    for g in range(groups):
        total = jnp.where(firsts[0] == g * GROUP, resids[0], 0.0)
        for k in range(1, per):
            total = total + jnp.where(firsts[k] == g * GROUP, resids[k], 0.0)
        placed.append(total)
    lagged = two_term_dot(jnp.concatenate(placed, 0), mask, 1)
    for g in range(groups):
        term = lagged[g * slots : (g + 1) * slots] * scale[g : g + 1]
        spread = skew_up(term, lags, rows).astype(BF16)
        spread_ref[:, g * GROUP * lags : (g + 1) * GROUP * lags] = spread
    table = table_ref[...].reshape(blocks * lags, cells)
    returned = jnp.dot(spread_ref[...], table, preferred_element_type=F32)
    own_ref[...] = returned[rows - slots :] + 0.5 * prior_ref[...] * flux_ref[...]
    core = lax.axis_index("stn")
    near = []
    for distance in range(1, rows // slots):
        start = rows - slots * (distance + 1)
        piece = returned[start : start + slots]
        near.append(jnp.where(shard >= distance, piece, jnp.zeros_like(piece)))
    for first in range(0, len(near), 2):
        if first + 1 < len(near):
            sent_refs[first][...] = jnp.where(core == 0, near[first + 1], near[first])
            sent_refs[first + 1][...] = jnp.where(core == 1, near[first + 1], near[first])
        else:
            sent_refs[first][...] = near[first].astype(sent_refs[first].dtype)


def order_kernel(slot_resid_ref, resid_ref, swap_float):
    per, slots, _ = slot_resid_ref.shape
    for k in range(per):
        swap_float[pl.ds(k, slots, stride=per), :] = slot_resid_ref[k]
    resid_ref[...] = swap_float[...].T


PARAMS = pltpu.CompilerParams(vmem_limit_bytes=12 * 1024 * 1024)
VMEM = pl.BlockSpec(memory_space=pltpu.VMEM)


def on_device(
    fluxes, prior_weight, footprint, block_scale, block_index, foot_length, observed, obs_weight
):
    slots, cells = fluxes.shape
    blocks, lags, _ = footprint.shape
    hours, stations = block_index.shape
    far = min(lags // slots, lax.axis_size("tm") - 1)
    rows = slots * (far + 1)
    own = pl.pallas_call(
        round_kernel,
        out_shape=jax.ShapeDtypeStruct((slots, cells), BF16),
        in_specs=[pl.BlockSpec(memory_space=pltpu.HBM)],
        out_specs=VMEM,
        scratch_shapes=[pltpu.VMEM((slots, cells), F32), pltpu.SemaphoreType.DMA],
        compiler_params=pltpu.CompilerParams(vmem_limit_bytes=2 * 1024 * 1024),
        cost_estimate=pl.CostEstimate(flops=2 * 10**10, bytes_accessed=10**5, transcendentals=0),
    )(pltpu.with_memory_space_constraint(fluxes, pltpu.HBM))
    moved = []
    for near in range(1, far + 1, 2):
        if near == far:
            moved.append(rolled(own, near))
        else:
            got = shared(own, near)
            moved += [got, swapped_sum(got, "stn")]
    per = hours // slots
    groups = blocks // GROUP
    by_hour = jax.ShapeDtypeStruct((per, slots, stations), F32)
    flops = 2 * blocks * lags * cells * rows
    nbytes = blocks * lags * cells * 2
    cost = pl.CostEstimate(flops=flops, bytes_accessed=nbytes, transcendentals=0)
    mine, scale, mask, first, seen, weight = pl.pallas_call(
        functools.partial(model_kernel, far),
        out_shape=[
            by_hour,
            jax.ShapeDtypeStruct((groups, GROUP * lags), F32),
            jax.ShapeDtypeStruct((GROUP * lags, GROUP * stations), BF16),
            jax.ShapeDtypeStruct((per, slots, GROUP * stations), jnp.int32),
            by_hour,
            by_hour,
        ],
        in_specs=[VMEM] * (far + 7),
        out_specs=[VMEM] * 6,
        scratch_shapes=[pltpu.VMEM((hours, stations), jnp.int32), pltpu.VMEM((2, hours, stations), F32)],
        compiler_params=PARAMS,
        cost_estimate=cost,
    )(*moved, own, footprint, block_scale, block_index.T, foot_length.reshape(1, stations), observed.T, obs_weight.T)
    other = swapped_sum(mine, "space")
    piece = jax.ShapeDtypeStruct((slots, cells), F32)
    sent = jax.ShapeDtypeStruct((slots, cells), BF16)
    resid, total, *back = pl.pallas_call(
        return_kernel,
        out_shape=[by_hour, piece] + [piece] * (far // 2 * 2) + [sent] * (far % 2),
        in_specs=[VMEM] * 10,
        out_specs=[VMEM] * (2 + far),
        scratch_shapes=[pltpu.VMEM((rows, blocks * lags), BF16)],
        compiler_params=PARAMS,
        cost_estimate=cost,
    )(mine, other, seen, weight, fluxes, prior_weight, footprint, scale, mask, first)
    arrived = []
    for near in range(1, far + 1, 2):
        if near == far:
            arrived.append(rolled(back[near - 1], -near))
        else:
            both = back[near - 1] + swapped_sum(back[near], "stn")
            arrived.append(shared(both.astype(BF16), near, -1))
    for piece in arrived[::-1]:
        total = total + piece
    resid = pl.pallas_call(
        order_kernel,
        out_shape=jax.ShapeDtypeStruct((stations, hours), F32),
        in_specs=[VMEM],
        out_specs=VMEM,
        scratch_shapes=[pltpu.VMEM((hours, stations), F32)],
        compiler_params=pltpu.CompilerParams(vmem_limit_bytes=2 * 1024 * 1024),
        cost_estimate=pl.CostEstimate(flops=10**6, bytes_accessed=10**4, transcendentals=0),
    )(resid)
    gradient = total + swapped_sum(total, "stn")
    return (resid.T, gradient)


def swapped_sum(x, axis):
    devices = lax.axis_size(axis)
    total = None
    for by in range(1, devices):
        moved = lax.ppermute(x, axis, [(i, (i + by) % devices) for i in range(devices)])
        total = moved if total is None else total + moved
    return total


def solution(mesh):
    placed = (
        P("tm", ("parts", "space")),
        P("tm", ("parts", "space")),
        P(("tm", "stn"), None, ("parts", "space")),
        P(("parts", "tm", "stn"), None),
        P(("parts", "tm"), "stn"),
        P(("parts", "stn")),
        P(("parts", "tm"), "stn"),
        P(("parts", "tm"), "stn"),
    )
    return jax.shard_map(
        on_device,
        mesh=mesh,
        in_specs=placed,
        out_specs=(P(("parts", "tm"), "stn"), P("tm", ("parts", "space"))),
        check_vma=False,
    )
```

```python
import functools

import jax
import jax.numpy as jnp
from jax import lax
from jax.experimental import pallas as pl
from jax.experimental.pallas import tpu as pltpu
from jax.sharding import PartitionSpec as P

F32 = jnp.float32
BF16 = jnp.bfloat16
GROUP = 4


def rolled(x, by):
    devices = lax.axis_size("tm")
    pairs = [(t * 2 + c, (t + by) % devices * 2 + 1 - c) for t in range(devices) for c in (0, 1)]
    return lax.ppermute(x, ("tm", "stn"), pairs)


def grouped(far, single):
    rest = [d for d in range(1, far + 1) if d != single or far % 2 == 0]
    groups = [(rest[i + 1], rest[i]) for i in range(0, len(rest), 2)]
    return groups + [(single,)] * (far % 2)


def grouped_fwd(far, single):
    return [g[::-1] for g in grouped(far, single)]


def shared(x, by):
    devices = lax.axis_size("tm")
    pairs = [
        (t * 2 + 1 - core, (t + by[core]) % devices * 2 + core)
        for t in range(devices)
        for core in (0, 1)
    ]
    return lax.ppermute(x, ("tm", "stn"), pairs)


def shared_back(x, by):
    devices = lax.axis_size("tm")
    pairs = [
        (t * 2 + core, (t + by[core]) % devices * 2 + core)
        for t in range(devices)
        for core in (0, 1)
    ]
    return lax.ppermute(x, ("tm", "stn"), pairs)


def reach_mask(len_ref, lags, stations):
    shape = (GROUP * lags, GROUP * stations)
    lengths = jnp.concatenate([len_ref[...]] * GROUP, axis=1)
    row = lax.broadcasted_iota(jnp.int32, shape, 0)
    col = lax.broadcasted_iota(jnp.int32, shape, 1)
    same = (row // lags) == (col // stations)
    return jnp.where(same & ((row % lags) < lengths), 1.0, 0.0).astype(BF16)


def lane_scale(scale_ref, groups):
    return jnp.concatenate(
        [scale_ref[pl.ds(i, groups, stride=GROUP), :] for i in range(GROUP)], axis=1
    )


def lag_bits(lags, rows):
    lag = lax.broadcasted_iota(jnp.int32, (rows, GROUP * lags), 1) % lags
    return lag


def two_term_dot(x, mask, contract):
    high = x.astype(BF16)
    low = (x - high.astype(F32)).astype(BF16)
    dims = (((1,), (contract,)), ((), ()))
    return lax.dot_general(high, mask, dims, preferred_element_type=F32) + lax.dot_general(
        low, mask, dims, preferred_element_type=F32
    )


def skew_down(x, lags, slots):
    need = slots + lags
    rows = x.shape[0]
    if rows < need:
        x = jnp.concatenate([jnp.zeros((need - rows, x.shape[1]), x.dtype), x], 0)
    step = lags // 2
    while step >= 8:
        keep = x.shape[0] - step
        bit = (lag_bits(lags, keep) & step) != 0
        x = jnp.where(bit, x[:keep], x[step:])
        step //= 2
    while step >= 1:
        bit = (lag_bits(lags, x.shape[0]) & step) != 0
        x = jnp.where(bit, pltpu.roll(x, step, 0), x)
        step //= 2
    return x[x.shape[0] - slots :]


def skew_up(x, lags, rows):
    slots, lanes = x.shape
    x = jnp.concatenate([jnp.zeros((8, lanes), x.dtype), x], 0)
    step = 1
    while step < 8:
        bit = (lag_bits(lags, x.shape[0]) & step) != 0
        x = jnp.where(bit, pltpu.roll(x, x.shape[0] - step, 0), x)
        step *= 2
    while step < lags:
        gap = jnp.zeros((step, lanes), x.dtype)
        bit = (lag_bits(lags, x.shape[0] + step) & step) != 0
        x = jnp.where(bit, jnp.concatenate([x, gap], 0), jnp.concatenate([gap, x], 0))
        step *= 2
    return x[x.shape[0] - rows :]


def round_kernel(flux_hbm, out_ref, flux_ref, sem):
    copy = pltpu.make_async_copy(flux_hbm, flux_ref, sem)
    copy.start()
    copy.wait()
    out_ref[...] = flux_ref[...].astype(out_ref.dtype)


def model_kernel(far, *refs):
    moved_refs = refs[: far]
    (own_ref, table_ref, block_scale_ref, index_ref, len_ref, seen_ref, weight_ref,
     out_ref, scale_ref, mask_ref, first_ref, slot_seen_ref, slot_weight_ref,
     swap_int, swap_float) = refs[far:]
    blocks, lags, cells = table_ref.shape
    per, slots, stations = out_ref.shape
    groups = blocks // GROUP
    core, shard = lax.axis_index("stn"), lax.axis_index("tm")
    pieces = {0: own_ref[...]}
    moved_refs = list(moved_refs)
    for group in grouped_fwd(far, 3):
        got = moved_refs.pop(0)[...]
        both = [got]
        if len(group) == 2:
            other = moved_refs.pop(0)[...]
            both = [jnp.where(core == i, got, other) for i in (0, 1)]
        for distance, piece in zip(group, both):
            pieces[distance] = jnp.where(shard >= distance, piece, jnp.zeros_like(piece))
    pieces = [pieces[d] for d in range(far + 1)]
    window = jnp.concatenate(pieces[::-1], 0)
    scale = lane_scale(block_scale_ref, groups)
    scale_ref[...] = scale
    mask = reach_mask(len_ref, lags, stations)
    mask_ref[...] = mask
    lane_block = lax.broadcasted_iota(jnp.int32, (slots, GROUP * stations), 1) // stations
    swap_int[...] = index_ref[...].T
    for k in range(per):
        index = swap_int[pl.ds(k, slots, stride=per), :]
        first_ref[k] = jnp.concatenate([index] * GROUP, axis=1) - lane_block
    for i, (source, target) in enumerate(((seen_ref, slot_seen_ref), (weight_ref, slot_weight_ref))):
        swap_float[i] = source[...].T
        for k in range(per):
            target[k] = swap_float[i, pl.ds(k, slots, stride=per), :]
    terms = []
    for g in range(groups):
        table = table_ref[g * GROUP : (g + 1) * GROUP].reshape(GROUP * lags, cells)
        products = lax.dot_general(
            table, window, (((1,), (1,)), ((), ())), preferred_element_type=F32
        ).T
        terms.append(skew_down(products, lags, slots) * scale[g : g + 1])
    sums = two_term_dot(jnp.concatenate(terms, 0), mask, 0)
    for k in range(per):
        first = first_ref[k]
        picked = jnp.zeros((slots, GROUP * stations), F32)
        for g in range(groups):
            picked = jnp.where(first == g * GROUP, sums[g * slots : (g + 1) * slots], picked)
        total = picked[:, :stations]
        for i in range(1, GROUP):
            total = total + picked[:, i * stations : (i + 1) * stations]
        out_ref[k] = total


def return_kernel(*refs):
    (mine_ref, other_ref, seen_ref, weight_ref, flux_ref, prior_ref, table_ref, scale_ref,
     mask_ref, first_ref, resid_ref, own_ref, *rest) = refs
    *sent_refs, spread_ref = rest
    blocks, lags, cells = table_ref.shape
    per, slots, stations = mine_ref.shape
    groups = blocks // GROUP
    rows = spread_ref.shape[0]
    shard = lax.axis_index("tm")
    scale = scale_ref[...]
    mask = mask_ref[...]
    firsts, resids = [], []
    for k in range(per):
        resid = weight_ref[k] * (mine_ref[k] + other_ref[k] - seen_ref[k])
        resid_ref[k] = resid
        resids.append(jnp.concatenate([resid] * GROUP, axis=1))
        firsts.append(first_ref[k])
    placed = []
    for g in range(groups):
        total = jnp.where(firsts[0] == g * GROUP, resids[0], 0.0)
        for k in range(1, per):
            total = total + jnp.where(firsts[k] == g * GROUP, resids[k], 0.0)
        placed.append(total)
    lagged = two_term_dot(jnp.concatenate(placed, 0), mask, 1)
    for g in range(groups):
        term = lagged[g * slots : (g + 1) * slots] * scale[g : g + 1]
        spread = skew_up(term, lags, rows).astype(BF16)
        spread_ref[:, g * GROUP * lags : (g + 1) * GROUP * lags] = spread
    table = table_ref[...].reshape(blocks * lags, cells)
    returned = jnp.dot(spread_ref[...], table, preferred_element_type=F32)
    own_ref[...] = returned[rows - slots :] + 0.5 * prior_ref[...] * flux_ref[...]
    core = lax.axis_index("stn")
    near = []
    for distance in range(1, rows // slots):
        start = rows - slots * (distance + 1)
        piece = returned[start : start + slots]
        near.append(jnp.where(shard >= distance, piece, jnp.zeros_like(piece)))
    sent_refs = list(sent_refs)
    for group in grouped(len(near), 3):
        if len(group) == 1:
            sent = sent_refs.pop(0)
            sent[...] = near[group[0] - 1].astype(sent.dtype)
        else:
            first, second = near[group[0] - 1], near[group[1] - 1]
            sent_refs.pop(0)[...] = jnp.where(core == 0, first, second)
            sent_refs.pop(0)[...] = jnp.where(core == 1, first, second)


def order_kernel(slot_resid_ref, resid_ref, swap_float):
    per, slots, _ = slot_resid_ref.shape
    for k in range(per):
        swap_float[pl.ds(k, slots, stride=per), :] = slot_resid_ref[k]
    resid_ref[...] = swap_float[...].T


PARAMS = pltpu.CompilerParams(vmem_limit_bytes=12 * 1024 * 1024)
VMEM = pl.BlockSpec(memory_space=pltpu.VMEM)


def on_device(
    fluxes, prior_weight, footprint, block_scale, block_index, foot_length, observed, obs_weight
):
    slots, cells = fluxes.shape
    blocks, lags, _ = footprint.shape
    hours, stations = block_index.shape
    far = min(lags // slots, lax.axis_size("tm") - 1)
    rows = slots * (far + 1)
    own = pl.pallas_call(
        round_kernel,
        out_shape=jax.ShapeDtypeStruct((slots, cells), BF16),
        in_specs=[pl.BlockSpec(memory_space=pltpu.HBM)],
        out_specs=VMEM,
        scratch_shapes=[pltpu.VMEM((slots, cells), F32), pltpu.SemaphoreType.DMA],
        compiler_params=pltpu.CompilerParams(vmem_limit_bytes=2 * 1024 * 1024),
        cost_estimate=pl.CostEstimate(flops=2 * 10**10, bytes_accessed=10**5, transcendentals=0),
    )(pltpu.with_memory_space_constraint(fluxes, pltpu.HBM))
    moved = []
    for group in grouped_fwd(far, 3):
        if len(group) == 1:
            moved.append(rolled(own, group[0]))
        else:
            got = shared(own, group)
            moved += [got, swapped_sum(got, "stn")]
    per = hours // slots
    groups = blocks // GROUP
    by_hour = jax.ShapeDtypeStruct((per, slots, stations), F32)
    flops = 2 * blocks * lags * cells * rows
    nbytes = blocks * lags * cells * 2
    cost = pl.CostEstimate(flops=flops, bytes_accessed=nbytes, transcendentals=0)
    mine, scale, mask, first, seen, weight = pl.pallas_call(
        functools.partial(model_kernel, far),
        out_shape=[
            by_hour,
            jax.ShapeDtypeStruct((groups, GROUP * lags), F32),
            jax.ShapeDtypeStruct((GROUP * lags, GROUP * stations), BF16),
            jax.ShapeDtypeStruct((per, slots, GROUP * stations), jnp.int32),
            by_hour,
            by_hour,
        ],
        in_specs=[VMEM] * (far + 7),
        out_specs=[VMEM] * 6,
        scratch_shapes=[pltpu.VMEM((hours, stations), jnp.int32), pltpu.VMEM((2, hours, stations), F32)],
        compiler_params=PARAMS,
        cost_estimate=cost,
    )(*moved, own, footprint, block_scale, block_index.T, foot_length.reshape(1, stations), observed.T, obs_weight.T)
    other = swapped_sum(mine, "space")
    piece = jax.ShapeDtypeStruct((slots, cells), F32)
    sent = jax.ShapeDtypeStruct((slots, cells), BF16)
    resid, total, *back = pl.pallas_call(
        return_kernel,
        out_shape=[by_hour, piece] + [piece] * (far // 2 * 2) + [sent] * (far % 2),
        in_specs=[VMEM] * 10,
        out_specs=[VMEM] * (2 + far),
        scratch_shapes=[pltpu.VMEM((rows, blocks * lags), BF16)],
        compiler_params=PARAMS,
        cost_estimate=cost,
    )(mine, other, seen, weight, fluxes, prior_weight, footprint, scale, mask, first)
    arrived = []
    for group in grouped(far, 3):
        if len(group) == 1:
            arrived.append(rolled(back.pop(0), -group[0]))
        else:
            both = back.pop(0) + swapped_sum(back.pop(0), "stn")
            arrived.append(shared_back(both.astype(BF16), [-d for d in group]))
    for piece in arrived[::-1]:
        total = total + piece
    resid = pl.pallas_call(
        order_kernel,
        out_shape=jax.ShapeDtypeStruct((stations, hours), F32),
        in_specs=[VMEM],
        out_specs=VMEM,
        scratch_shapes=[pltpu.VMEM((hours, stations), F32)],
        compiler_params=pltpu.CompilerParams(vmem_limit_bytes=2 * 1024 * 1024),
        cost_estimate=pl.CostEstimate(flops=10**6, bytes_accessed=10**4, transcendentals=0),
    )(resid)
    gradient = total + swapped_sum(total, "stn")
    return (resid.T, gradient)


def swapped_sum(x, axis):
    devices = lax.axis_size(axis)
    total = None
    for by in range(1, devices):
        moved = lax.ppermute(x, axis, [(i, (i + by) % devices) for i in range(devices)])
        total = moved if total is None else total + moved
    return total


def solution(mesh):
    placed = (
        P("tm", ("parts", "space")),
        P("tm", ("parts", "space")),
        P(("tm", "stn"), None, ("parts", "space")),
        P(("parts", "tm", "stn"), None),
        P(("parts", "tm"), "stn"),
        P(("parts", "stn")),
        P(("parts", "tm"), "stn"),
        P(("parts", "tm"), "stn"),
    )
    return jax.shard_map(
        on_device,
        mesh=mesh,
        in_specs=placed,
        out_specs=(P(("parts", "tm"), "stn"), P("tm", ("parts", "space"))),
        check_vma=False,
    )
```

```python
import functools

import jax
import jax.numpy as jnp
from jax import lax
from jax.experimental import pallas as pl
from jax.experimental.pallas import tpu as pltpu
from jax.sharding import PartitionSpec as P

F32 = jnp.float32
BF16 = jnp.bfloat16
GROUP = 4


def rolled(x, by):
    devices = lax.axis_size("tm")
    pairs = [(t * 2 + c, (t + by) % devices * 2 + 1 - c) for t in range(devices) for c in (0, 1)]
    return lax.ppermute(x, ("tm", "stn"), pairs)


def grouped(far, single):
    rest = [d for d in range(1, far + 1) if d != single or far % 2 == 0]
    groups = [(rest[i + 1], rest[i]) for i in range(0, len(rest), 2)]
    return groups + [(single,)] * (far % 2)


def grouped_fwd(far, single):
    return [g[::-1] for g in grouped(far, single)]


def shared(x, by):
    devices = lax.axis_size("tm")
    pairs = [
        (t * 2 + 1 - core, (t + by[core]) % devices * 2 + core)
        for t in range(devices)
        for core in (0, 1)
    ]
    return lax.ppermute(x, ("tm", "stn"), pairs)


def shared_back(x, by):
    devices = lax.axis_size("tm")
    pairs = [
        (t * 2 + core, (t + by[core]) % devices * 2 + core)
        for t in range(devices)
        for core in (0, 1)
    ]
    return lax.ppermute(x, ("tm", "stn"), pairs)


def reach_mask(len_ref, lags, stations):
    shape = (GROUP * lags, GROUP * stations)
    lengths = jnp.concatenate([len_ref[...]] * GROUP, axis=1)
    row = lax.broadcasted_iota(jnp.int32, shape, 0)
    col = lax.broadcasted_iota(jnp.int32, shape, 1)
    same = (row // lags) == (col // stations)
    return jnp.where(same & ((row % lags) < lengths), 1.0, 0.0).astype(BF16)


def lane_scale(scale_ref, groups):
    return jnp.concatenate(
        [scale_ref[pl.ds(i, groups, stride=GROUP), :] for i in range(GROUP)], axis=1
    )


def lag_bits(lags, rows):
    lag = lax.broadcasted_iota(jnp.int32, (rows, GROUP * lags), 1) % lags
    return lag


def two_term_dot(x, mask, contract):
    high = x.astype(BF16)
    low = (x - high.astype(F32)).astype(BF16)
    dims = (((1,), (contract,)), ((), ()))
    return lax.dot_general(high, mask, dims, preferred_element_type=F32) + lax.dot_general(
        low, mask, dims, preferred_element_type=F32
    )


def skew_down(x, lags, slots):
    need = slots + lags
    rows = x.shape[0]
    if rows < need:
        x = jnp.concatenate([jnp.zeros((need - rows, x.shape[1]), x.dtype), x], 0)
    step = lags // 2
    while step >= 8:
        keep = x.shape[0] - step
        bit = (lag_bits(lags, keep) & step) != 0
        x = jnp.where(bit, x[:keep], x[step:])
        step //= 2
    while step >= 1:
        bit = (lag_bits(lags, x.shape[0]) & step) != 0
        x = jnp.where(bit, pltpu.roll(x, step, 0), x)
        step //= 2
    return x[x.shape[0] - slots :]


def skew_up(x, lags, rows):
    slots, lanes = x.shape
    x = jnp.concatenate([jnp.zeros((8, lanes), x.dtype), x], 0)
    step = 1
    while step < 8:
        bit = (lag_bits(lags, x.shape[0]) & step) != 0
        x = jnp.where(bit, pltpu.roll(x, x.shape[0] - step, 0), x)
        step *= 2
    while step < lags:
        gap = jnp.zeros((step, lanes), x.dtype)
        bit = (lag_bits(lags, x.shape[0] + step) & step) != 0
        x = jnp.where(bit, jnp.concatenate([x, gap], 0), jnp.concatenate([gap, x], 0))
        step *= 2
    return x[x.shape[0] - rows :]


def round_kernel(flux_hbm, out_ref, flux_ref, sem):
    copy = pltpu.make_async_copy(flux_hbm, flux_ref, sem)
    copy.start()
    copy.wait()
    out_ref[...] = flux_ref[...].astype(out_ref.dtype)


def model_kernel(far, *refs):
    moved_refs = refs[: far]
    (own_ref, table_ref, block_scale_ref, index_ref, len_ref, seen_ref, weight_ref,
     out_ref, scale_ref, mask_ref, first_ref, slot_seen_ref, slot_weight_ref,
     swap_int, swap_float) = refs[far:]
    blocks, lags, cells = table_ref.shape
    per, slots, stations = out_ref.shape
    groups = blocks // GROUP
    core, shard = lax.axis_index("stn"), lax.axis_index("tm")
    pieces = {0: own_ref[...]}
    moved_refs = list(moved_refs)
    for group in grouped_fwd(far, 3):
        got = moved_refs.pop(0)[...]
        both = [got]
        if len(group) == 2:
            other = moved_refs.pop(0)[...]
            both = [jnp.where(core == i, got, other) for i in (0, 1)]
        for distance, piece in zip(group, both):
            pieces[distance] = jnp.where(shard >= distance, piece, jnp.zeros_like(piece))
    pieces = [pieces[d] for d in range(far + 1)]
    window = jnp.concatenate(pieces[::-1], 0)
    scale = lane_scale(block_scale_ref, groups)
    scale_ref[...] = scale
    mask = reach_mask(len_ref, lags, stations)
    mask_ref[...] = mask
    lane_block = lax.broadcasted_iota(jnp.int32, (slots, GROUP * stations), 1) // stations
    swap_int[...] = index_ref[...].T
    for k in range(per):
        index = swap_int[pl.ds(k, slots, stride=per), :]
        first_ref[k] = jnp.concatenate([index] * GROUP, axis=1) - lane_block
    for i, (source, target) in enumerate(((seen_ref, slot_seen_ref), (weight_ref, slot_weight_ref))):
        swap_float[i] = source[...].T
        for k in range(per):
            target[k] = swap_float[i, pl.ds(k, slots, stride=per), :]
    terms = []
    for g in range(groups):
        table = table_ref[g * GROUP : (g + 1) * GROUP].reshape(GROUP * lags, cells)
        products = lax.dot_general(
            table, window, (((1,), (1,)), ((), ())), preferred_element_type=F32
        ).T
        terms.append(skew_down(products, lags, slots) * scale[g : g + 1])
    sums = two_term_dot(jnp.concatenate(terms, 0), mask, 0)
    for k in range(per):
        first = first_ref[k]
        picked = jnp.zeros((slots, GROUP * stations), F32)
        for g in range(groups):
            picked = jnp.where(first == g * GROUP, sums[g * slots : (g + 1) * slots], picked)
        total = picked[:, :stations]
        for i in range(1, GROUP):
            total = total + picked[:, i * stations : (i + 1) * stations]
        out_ref[k] = total


def return_kernel(*refs):
    (mine_ref, other_ref, seen_ref, weight_ref, flux_ref, prior_ref, table_ref, scale_ref,
     mask_ref, first_ref, resid_ref, own_ref, *rest) = refs
    *sent_refs, spread_ref = rest
    blocks, lags, cells = table_ref.shape
    per, slots, stations = mine_ref.shape
    groups = blocks // GROUP
    rows = spread_ref.shape[0]
    shard = lax.axis_index("tm")
    scale = scale_ref[...]
    mask = mask_ref[...]
    firsts, resids = [], []
    for k in range(per):
        resid = weight_ref[k] * (mine_ref[k] + other_ref[k] - seen_ref[k])
        resid_ref[k] = resid
        resids.append(jnp.concatenate([resid] * GROUP, axis=1))
        firsts.append(first_ref[k])
    placed = []
    for g in range(groups):
        total = jnp.where(firsts[0] == g * GROUP, resids[0], 0.0)
        for k in range(1, per):
            total = total + jnp.where(firsts[k] == g * GROUP, resids[k], 0.0)
        placed.append(total)
    lagged = two_term_dot(jnp.concatenate(placed, 0), mask, 1)
    for g in range(groups):
        term = lagged[g * slots : (g + 1) * slots] * scale[g : g + 1]
        spread = skew_up(term, lags, rows).astype(BF16)
        spread_ref[:, g * GROUP * lags : (g + 1) * GROUP * lags] = spread
    table = table_ref[...].reshape(blocks * lags, cells)
    returned = jnp.dot(spread_ref[...], table, preferred_element_type=F32)
    own_ref[...] = returned[rows - slots :] + 0.5 * prior_ref[...] * flux_ref[...]
    core = lax.axis_index("stn")
    near = []
    for distance in range(1, rows // slots):
        start = rows - slots * (distance + 1)
        piece = returned[start : start + slots]
        near.append(jnp.where(shard >= distance, piece, jnp.zeros_like(piece)))
    sent_refs = list(sent_refs)
    for group in grouped_fwd(len(near), 3):
        if len(group) == 1:
            sent = sent_refs.pop(0)
            sent[...] = near[group[0] - 1].astype(sent.dtype)
        else:
            first, second = near[group[0] - 1], near[group[1] - 1]
            sent_refs.pop(0)[...] = jnp.where(core == 1, first, second)
            sent_refs.pop(0)[...] = jnp.where(core == 0, first, second)


def order_kernel(slot_resid_ref, resid_ref, swap_float):
    per, slots, _ = slot_resid_ref.shape
    for k in range(per):
        swap_float[pl.ds(k, slots, stride=per), :] = slot_resid_ref[k]
    resid_ref[...] = swap_float[...].T


PARAMS = pltpu.CompilerParams(vmem_limit_bytes=12 * 1024 * 1024)
VMEM = pl.BlockSpec(memory_space=pltpu.VMEM)


def on_device(
    fluxes, prior_weight, footprint, block_scale, block_index, foot_length, observed, obs_weight
):
    slots, cells = fluxes.shape
    blocks, lags, _ = footprint.shape
    hours, stations = block_index.shape
    far = min(lags // slots, lax.axis_size("tm") - 1)
    rows = slots * (far + 1)
    own = pl.pallas_call(
        round_kernel,
        out_shape=jax.ShapeDtypeStruct((slots, cells), BF16),
        in_specs=[pl.BlockSpec(memory_space=pltpu.HBM)],
        out_specs=VMEM,
        scratch_shapes=[pltpu.VMEM((slots, cells), F32), pltpu.SemaphoreType.DMA],
        compiler_params=pltpu.CompilerParams(vmem_limit_bytes=2 * 1024 * 1024),
        cost_estimate=pl.CostEstimate(flops=2 * 10**10, bytes_accessed=10**5, transcendentals=0),
    )(pltpu.with_memory_space_constraint(fluxes, pltpu.HBM))
    moved = []
    for group in grouped_fwd(far, 3):
        if len(group) == 1:
            moved.append(rolled(own, group[0]))
        else:
            got = shared(own, group)
            moved += [got, swapped_sum(got, "stn")]
    per = hours // slots
    groups = blocks // GROUP
    by_hour = jax.ShapeDtypeStruct((per, slots, stations), F32)
    flops = 2 * blocks * lags * cells * rows
    nbytes = blocks * lags * cells * 2
    cost = pl.CostEstimate(flops=flops, bytes_accessed=nbytes, transcendentals=0)
    mine, scale, mask, first, seen, weight = pl.pallas_call(
        functools.partial(model_kernel, far),
        out_shape=[
            by_hour,
            jax.ShapeDtypeStruct((groups, GROUP * lags), F32),
            jax.ShapeDtypeStruct((GROUP * lags, GROUP * stations), BF16),
            jax.ShapeDtypeStruct((per, slots, GROUP * stations), jnp.int32),
            by_hour,
            by_hour,
        ],
        in_specs=[VMEM] * (far + 7),
        out_specs=[VMEM] * 6,
        scratch_shapes=[pltpu.VMEM((hours, stations), jnp.int32), pltpu.VMEM((2, hours, stations), F32)],
        compiler_params=PARAMS,
        cost_estimate=cost,
    )(*moved, own, footprint, block_scale, block_index.T, foot_length.reshape(1, stations), observed.T, obs_weight.T)
    other = swapped_sum(mine, "space")
    piece = jax.ShapeDtypeStruct((slots, cells), F32)
    sent = jax.ShapeDtypeStruct((slots, cells), BF16)
    resid, total, *back = pl.pallas_call(
        return_kernel,
        out_shape=[by_hour, piece] + [piece] * (far // 2 * 2) + [sent] * (far % 2),
        in_specs=[VMEM] * 10,
        out_specs=[VMEM] * (2 + far),
        scratch_shapes=[pltpu.VMEM((rows, blocks * lags), BF16)],
        compiler_params=PARAMS,
        cost_estimate=cost,
    )(mine, other, seen, weight, fluxes, prior_weight, footprint, scale, mask, first)
    arrived = []
    for group in grouped_fwd(far, 3):
        if len(group) == 1:
            arrived.append(rolled(back.pop(0), -group[0]))
        else:
            both = back.pop(0) + swapped_sum(back.pop(0), "stn")
            arrived.append(shared(both.astype(BF16), [-d for d in group]))
    for piece in arrived[::-1]:
        total = total + piece
    resid = pl.pallas_call(
        order_kernel,
        out_shape=jax.ShapeDtypeStruct((stations, hours), F32),
        in_specs=[VMEM],
        out_specs=VMEM,
        scratch_shapes=[pltpu.VMEM((hours, stations), F32)],
        compiler_params=pltpu.CompilerParams(vmem_limit_bytes=2 * 1024 * 1024),
        cost_estimate=pl.CostEstimate(flops=10**6, bytes_accessed=10**4, transcendentals=0),
    )(resid)
    gradient = total + swapped_sum(total, "stn")
    return (resid.T, gradient)


def swapped_sum(x, axis):
    devices = lax.axis_size(axis)
    total = None
    for by in range(1, devices):
        moved = lax.ppermute(x, axis, [(i, (i + by) % devices) for i in range(devices)])
        total = moved if total is None else total + moved
    return jnp.zeros_like(x) if total is None else total


def solution(mesh):
    placed = (
        P("tm", ("parts", "space")),
        P("tm", ("parts", "space")),
        P(("tm", "stn"), None, ("parts", "space")),
        P(("parts", "tm", "stn"), None),
        P(("parts", "tm"), "stn"),
        P(("parts", "stn")),
        P(("parts", "tm"), "stn"),
        P(("parts", "tm"), "stn"),
    )
    return jax.shard_map(
        on_device,
        mesh=mesh,
        in_specs=placed,
        out_specs=(P(("parts", "tm"), "stn"), P("tm", ("parts", "space"))),
        check_vma=False,
    )
```

```python
import functools

import jax
import jax.numpy as jnp
from jax import lax
from jax.experimental import pallas as pl
from jax.experimental.pallas import tpu as pltpu
from jax.sharding import PartitionSpec as P

F32 = jnp.float32
BF16 = jnp.bfloat16
GROUP = 4


def rolled(x, by):
    devices = lax.axis_size("tm")
    pairs = [(t * 2 + c, (t + by) % devices * 2 + 1 - c) for t in range(devices) for c in (0, 1)]
    return lax.ppermute(x, ("tm", "stn"), pairs)


def grouped(far, single):
    rest = [d for d in range(1, far + 1) if d != single or far % 2 == 0]
    groups = [(rest[i + 1], rest[i]) for i in range(0, len(rest), 2)]
    return groups + [(single,)] * (far % 2)


def grouped_fwd(far, single):
    return [g[::-1] for g in grouped(far, single)]


def shared(x, by):
    devices = lax.axis_size("tm")
    pairs = [
        (t * 2 + 1 - core, (t + by[core]) % devices * 2 + core)
        for t in range(devices)
        for core in (0, 1)
    ]
    return lax.ppermute(x, ("tm", "stn"), pairs)


def shared_back(x, by):
    devices = lax.axis_size("tm")
    pairs = [
        (t * 2 + core, (t + by[core]) % devices * 2 + core)
        for t in range(devices)
        for core in (0, 1)
    ]
    return lax.ppermute(x, ("tm", "stn"), pairs)


def reach_mask(len_ref, lags, stations, per, wide):
    shape = (GROUP * lags, wide)
    lengths = jnp.concatenate([len_ref[...]] * (wide // stations), axis=1)
    row = lax.broadcasted_iota(jnp.int32, shape, 0)
    col = lax.broadcasted_iota(jnp.int32, shape, 1)
    part = GROUP * stations
    same = ((row // lags) == (col % part // stations)) & (col < per * part)
    return jnp.where(same & ((row % lags) < lengths), 1.0, 0.0).astype(BF16)


def lane_scale(scale_ref, groups):
    return jnp.concatenate(
        [scale_ref[pl.ds(i, groups, stride=GROUP), :] for i in range(GROUP)], axis=1
    )


def lag_bits(lags, rows):
    lag = lax.broadcasted_iota(jnp.int32, (rows, GROUP * lags), 1) % lags
    return lag


def two_term_dot(x, mask, contract):
    high = x.astype(BF16)
    low = (x - high.astype(F32)).astype(BF16)
    dims = (((1,), (contract,)), ((), ()))
    return lax.dot_general(high, mask, dims, preferred_element_type=F32) + lax.dot_general(
        low, mask, dims, preferred_element_type=F32
    )


def skew_down(x, lags, slots):
    need = slots + lags
    rows = x.shape[0]
    if rows < need:
        x = jnp.concatenate([jnp.zeros((need - rows, x.shape[1]), x.dtype), x], 0)
    step = lags // 2
    while step >= 8:
        keep = x.shape[0] - step
        bit = (lag_bits(lags, keep) & step) != 0
        x = jnp.where(bit, x[:keep], x[step:])
        step //= 2
    while step >= 1:
        bit = (lag_bits(lags, x.shape[0]) & step) != 0
        x = jnp.where(bit, pltpu.roll(x, step, 0), x)
        step //= 2
    return x[x.shape[0] - slots :]


def skew_up(x, lags, rows):
    slots, lanes = x.shape
    x = jnp.concatenate([jnp.zeros((8, lanes), x.dtype), x], 0)
    step = 1
    while step < 8:
        bit = (lag_bits(lags, x.shape[0]) & step) != 0
        x = jnp.where(bit, pltpu.roll(x, x.shape[0] - step, 0), x)
        step *= 2
    while step < lags:
        gap = jnp.zeros((step, lanes), x.dtype)
        bit = (lag_bits(lags, x.shape[0] + step) & step) != 0
        x = jnp.where(bit, jnp.concatenate([x, gap], 0), jnp.concatenate([gap, x], 0))
        step *= 2
    return x[x.shape[0] - rows :]


def round_kernel(flux_ref, out_ref):
    out_ref[...] = flux_ref[...].astype(out_ref.dtype)


def model_kernel(far, *refs):
    moved_refs = refs[: far]
    (own_ref, table_ref, block_scale_ref, index_ref, len_ref, seen_ref, weight_ref,
     out_ref, scale_ref, mask_ref, first_ref, slot_seen_ref, slot_weight_ref,
     swap_int, swap_float) = refs[far:]
    blocks, lags, cells = table_ref.shape
    slots, wide = out_ref.shape
    stations, hours = index_ref.shape
    per, part = hours // slots, GROUP * stations
    groups = blocks // GROUP
    core, shard = lax.axis_index("stn"), lax.axis_index("tm")
    pieces = {0: own_ref[...]}
    moved_refs = list(moved_refs)
    for group in grouped_fwd(far, 3):
        got = moved_refs.pop(0)[...]
        both = [got]
        if len(group) == 2:
            other = moved_refs.pop(0)[...]
            both = [jnp.where(core == i, got, other) for i in (0, 1)]
        for distance, piece in zip(group, both):
            pieces[distance] = jnp.where(shard >= distance, piece, jnp.zeros_like(piece))
    pieces = [pieces[d] for d in range(far + 1)]
    window = jnp.concatenate(pieces[::-1], 0)
    scale = lane_scale(block_scale_ref, groups)
    scale_ref[...] = scale
    mask = reach_mask(len_ref, lags, stations, per, wide)
    mask_ref[...] = mask
    lane = lax.broadcasted_iota(jnp.int32, (slots, wide), 1)
    rest = wide - per * part
    swap_int[...] = index_ref[...].T
    pieces = []
    for k in range(per):
        pieces += [swap_int[pl.ds(k, slots, stride=per), :]] * GROUP
    pieces += [jnp.zeros((slots, rest), jnp.int32)] if rest else []
    first = jnp.concatenate(pieces, axis=1) - lane % part // stations
    first_ref[...] = first
    for i, (source, target) in enumerate(((seen_ref, slot_seen_ref), (weight_ref, slot_weight_ref))):
        swap_float[i] = source[...].T
        pieces = []
        for k in range(per):
            pieces.append(swap_float[i, pl.ds(k, slots, stride=per), :])
            pieces.append(jnp.zeros((slots, part - stations), F32))
        pieces += [jnp.zeros((slots, rest), F32)] if rest else []
        target[...] = jnp.concatenate(pieces, axis=1)
    terms = []
    for g in range(groups):
        table = table_ref[g * GROUP : (g + 1) * GROUP].reshape(GROUP * lags, cells)
        products = lax.dot_general(
            table, window, (((1,), (1,)), ((), ())), preferred_element_type=F32
        ).T
        terms.append(skew_down(products, lags, slots) * scale[g : g + 1])
    sums = two_term_dot(jnp.concatenate(terms, 0), mask, 0)
    picked = jnp.zeros((slots, wide), F32)
    for g in range(groups):
        picked = jnp.where(first == g * GROUP, sums[g * slots : (g + 1) * slots], picked)
    total = picked
    for i in range(1, GROUP):
        total = total + pltpu.roll(picked, wide - i * stations, 1)
    out_ref[...] = total


def return_kernel(per, stations, *refs):
    (mine_ref, other_ref, seen_ref, weight_ref, flux_ref, prior_ref, table_ref, scale_ref,
     mask_ref, first_ref, resid_ref, own_ref, *rest) = refs
    *sent_refs, spread_ref = rest
    blocks, lags, cells = table_ref.shape
    slots, wide = mine_ref.shape
    part = GROUP * stations
    groups = blocks // GROUP
    rows = spread_ref.shape[0]
    shard = lax.axis_index("tm")
    scale = scale_ref[...]
    mask = mask_ref[...]
    first = first_ref[...]
    lane = lax.broadcasted_iota(jnp.int32, (slots, wide), 1)
    held = (lane % part < stations) & (lane < per * part)
    resid = jnp.where(held, weight_ref[...] * (mine_ref[...] + other_ref[...] - seen_ref[...]), 0.0)
    resid_ref[...] = resid
    spreading = resid
    for i in range(1, GROUP):
        spreading = spreading + pltpu.roll(resid, i * stations, 1)
    placed = [jnp.where(first == g * GROUP, spreading, 0.0) for g in range(groups)]
    lagged = two_term_dot(jnp.concatenate(placed, 0), mask, 1)
    for g in range(groups):
        term = lagged[g * slots : (g + 1) * slots] * scale[g : g + 1]
        spread = skew_up(term, lags, rows).astype(BF16)
        spread_ref[:, g * GROUP * lags : (g + 1) * GROUP * lags] = spread
    table = table_ref[...].reshape(blocks * lags, cells)
    returned = jnp.dot(spread_ref[...], table, preferred_element_type=F32)
    own_ref[...] = returned[rows - slots :] + 0.5 * prior_ref[...] * flux_ref[...]
    core = lax.axis_index("stn")
    near = []
    for distance in range(1, rows // slots):
        start = rows - slots * (distance + 1)
        piece = returned[start : start + slots]
        near.append(jnp.where(shard >= distance, piece, jnp.zeros_like(piece)))
    sent_refs = list(sent_refs)
    for group in grouped_fwd(len(near), 3):
        if len(group) == 1:
            sent = sent_refs.pop(0)
            sent[...] = near[group[0] - 1].astype(sent.dtype)
        else:
            first, second = near[group[0] - 1], near[group[1] - 1]
            sent_refs.pop(0)[...] = jnp.where(core == 1, first, second)
            sent_refs.pop(0)[...] = jnp.where(core == 0, first, second)


def order_kernel(slot_resid_ref, resid_ref, swap_float):
    stations, hours = resid_ref.shape
    slots, part = slot_resid_ref.shape[0], GROUP * stations
    per = hours // slots
    for k in range(per):
        swap_float[pl.ds(k, slots, stride=per), :] = slot_resid_ref[:, k * part : k * part + stations]
    resid_ref[...] = swap_float[...].T


PARAMS = pltpu.CompilerParams(vmem_limit_bytes=12 * 1024 * 1024)
VMEM = pl.BlockSpec(memory_space=pltpu.VMEM)


def on_device(
    fluxes, prior_weight, footprint, block_scale, block_index, foot_length, observed, obs_weight
):
    slots, cells = fluxes.shape
    blocks, lags, _ = footprint.shape
    hours, stations = block_index.shape
    far = min(lags // slots, lax.axis_size("tm") - 1)
    rows = slots * (far + 1)
    own = fluxes
    for flops in (10**4, 2 * 10**10):
        own = pl.pallas_call(
            round_kernel,
            out_shape=jax.ShapeDtypeStruct((slots, cells), BF16),
            in_specs=[VMEM],
            out_specs=VMEM,
            compiler_params=pltpu.CompilerParams(vmem_limit_bytes=2 * 1024 * 1024),
            cost_estimate=pl.CostEstimate(flops=flops, bytes_accessed=10**5, transcendentals=0),
        )(own)
    moved = []
    for group in grouped_fwd(far, 3):
        if len(group) == 1:
            moved.append(rolled(own, group[0]))
        else:
            got = shared(own, group)
            moved += [got, swapped_sum(got, "stn")]
    per = hours // slots
    groups = blocks // GROUP
    wide = -(-per * GROUP * stations // 128) * 128
    by_hour = jax.ShapeDtypeStruct((slots, wide), F32)
    flops = 2 * blocks * lags * cells * rows
    nbytes = blocks * lags * cells * 2
    cost = pl.CostEstimate(flops=flops, bytes_accessed=nbytes, transcendentals=0)
    mine, scale, mask, first, seen, weight = pl.pallas_call(
        functools.partial(model_kernel, far),
        out_shape=[
            by_hour,
            jax.ShapeDtypeStruct((groups, GROUP * lags), F32),
            jax.ShapeDtypeStruct((GROUP * lags, wide), BF16),
            jax.ShapeDtypeStruct((slots, wide), jnp.int32),
            by_hour,
            by_hour,
        ],
        in_specs=[VMEM] * (far + 7),
        out_specs=[VMEM] * 6,
        scratch_shapes=[pltpu.VMEM((hours, stations), jnp.int32), pltpu.VMEM((2, hours, stations), F32)],
        compiler_params=PARAMS,
        cost_estimate=cost,
    )(*moved, own, footprint, block_scale, block_index.T, foot_length.reshape(1, stations), observed.T, obs_weight.T)
    other = swapped_sum(mine, "space")
    piece = jax.ShapeDtypeStruct((slots, cells), F32)
    sent = jax.ShapeDtypeStruct((slots, cells), BF16)
    resid, total, *back = pl.pallas_call(
        functools.partial(return_kernel, per, stations),
        out_shape=[by_hour, piece] + [piece] * (far // 2 * 2) + [sent] * (far % 2),
        in_specs=[VMEM] * 10,
        out_specs=[VMEM] * (2 + far),
        scratch_shapes=[pltpu.VMEM((rows, blocks * lags), BF16)],
        compiler_params=PARAMS,
        cost_estimate=cost,
    )(mine, other, seen, weight, fluxes, prior_weight, footprint, scale, mask, first)
    arrived = []
    for group in grouped_fwd(far, 3):
        if len(group) == 1:
            arrived.append(rolled(back.pop(0), -group[0]))
        else:
            both = back.pop(0) + swapped_sum(back.pop(0), "stn")
            arrived.append(shared(both.astype(BF16), [-d for d in group]))
    for piece in arrived[::-1]:
        total = total + piece
    resid = pl.pallas_call(
        order_kernel,
        out_shape=jax.ShapeDtypeStruct((stations, hours), F32),
        in_specs=[VMEM],
        out_specs=VMEM,
        scratch_shapes=[pltpu.VMEM((hours, stations), F32)],
        compiler_params=pltpu.CompilerParams(vmem_limit_bytes=2 * 1024 * 1024),
        cost_estimate=pl.CostEstimate(flops=10**6, bytes_accessed=10**4, transcendentals=0),
    )(resid)
    gradient = total + swapped_sum(total, "stn")
    return (resid.T, gradient)


def swapped_sum(x, axis):
    devices = lax.axis_size(axis)
    total = None
    for by in range(1, devices):
        moved = lax.ppermute(x, axis, [(i, (i + by) % devices) for i in range(devices)])
        total = moved if total is None else total + moved
    return jnp.zeros_like(x) if total is None else total


def solution(mesh):
    placed = (
        P("tm", ("parts", "space")),
        P("tm", ("parts", "space")),
        P(("tm", "stn"), None, ("parts", "space")),
        P(("parts", "tm", "stn"), None),
        P(("parts", "tm"), "stn"),
        P(("parts", "stn")),
        P(("parts", "tm"), "stn"),
        P(("parts", "tm"), "stn"),
    )
    return jax.shard_map(
        on_device,
        mesh=mesh,
        in_specs=placed,
        out_specs=(P(("parts", "tm"), "stn"), P("tm", ("parts", "space"))),
        check_vma=False,
    )
```

```python
import functools

import jax
import jax.numpy as jnp
from jax import lax
from jax.experimental import pallas as pl
from jax.experimental.pallas import tpu as pltpu
from jax.sharding import PartitionSpec as P

F32 = jnp.float32
BF16 = jnp.bfloat16
GROUP = 4


def rolled(x, by):
    devices = lax.axis_size("tm")
    pairs = [(t * 2 + c, (t + by) % devices * 2 + 1 - c) for t in range(devices) for c in (0, 1)]
    return lax.ppermute(x, ("tm", "stn"), pairs)


def straight(x, by):
    devices = lax.axis_size("tm")
    return lax.ppermute(x, "tm", [(t, (t + by) % devices) for t in range(devices)])


def grouped(far, single):
    rest = [d for d in range(1, far + 1) if d != single or far % 2 == 0]
    groups = [(rest[i + 1], rest[i]) for i in range(0, len(rest), 2)]
    return groups + [(single,)] * (far % 2)


def grouped_fwd(far, single):
    return [g[::-1] for g in grouped(far, single)]


def shared(x, by):
    devices = lax.axis_size("tm")
    pairs = [
        (t * 2 + 1 - core, (t + by[core]) % devices * 2 + core)
        for t in range(devices)
        for core in (0, 1)
    ]
    return lax.ppermute(x, ("tm", "stn"), pairs)


def reach_mask(len_ref, lags, stations, per, wide):
    shape = (GROUP * lags, wide)
    lengths = jnp.concatenate([len_ref[...]] * (wide // stations), axis=1)
    row = lax.broadcasted_iota(jnp.int32, shape, 0)
    col = lax.broadcasted_iota(jnp.int32, shape, 1)
    part = GROUP * stations
    same = ((row // lags) == (col % part // stations)) & (col < per * part)
    return jnp.where(same & ((row % lags) < lengths), 1.0, 0.0).astype(BF16)


def lane_scale(scale_ref, groups):
    return jnp.concatenate(
        [scale_ref[pl.ds(i, groups, stride=GROUP), :] for i in range(GROUP)], axis=1
    )


def lag_bits(lags, rows):
    lag = lax.broadcasted_iota(jnp.int32, (rows, GROUP * lags), 1) % lags
    return lag


def two_term_dot(x, mask, contract):
    high = x.astype(BF16)
    low = (x - high.astype(F32)).astype(BF16)
    dims = (((1,), (contract,)), ((), ()))
    return lax.dot_general(high, mask, dims, preferred_element_type=F32) + lax.dot_general(
        low, mask, dims, preferred_element_type=F32
    )


def skew_down(x, lags, slots):
    need = slots + lags
    rows = x.shape[0]
    if rows < need:
        x = jnp.concatenate([jnp.zeros((need - rows, x.shape[1]), x.dtype), x], 0)
    step = lags // 2
    while step >= 8:
        keep = x.shape[0] - step
        bit = (lag_bits(lags, keep) & step) != 0
        x = jnp.where(bit, x[:keep], x[step:])
        step //= 2
    while step >= 1:
        bit = (lag_bits(lags, x.shape[0]) & step) != 0
        x = jnp.where(bit, pltpu.roll(x, step, 0), x)
        step //= 2
    return x[x.shape[0] - slots :]


def skew_up(x, lags, rows):
    slots, lanes = x.shape
    x = jnp.concatenate([jnp.zeros((8, lanes), x.dtype), x], 0)
    step = 1
    while step < 8:
        bit = (lag_bits(lags, x.shape[0]) & step) != 0
        x = jnp.where(bit, pltpu.roll(x, x.shape[0] - step, 0), x)
        step *= 2
    while step < lags:
        gap = jnp.zeros((step, lanes), x.dtype)
        bit = (lag_bits(lags, x.shape[0] + step) & step) != 0
        x = jnp.where(bit, jnp.concatenate([x, gap], 0), jnp.concatenate([gap, x], 0))
        step *= 2
    return x[x.shape[0] - rows :]


def round_kernel(flux_ref, out_ref):
    out_ref[...] = flux_ref[...].astype(out_ref.dtype)


def model_kernel(far, *refs):
    moved_refs = refs[: far]
    (own_ref, table_ref, block_scale_ref, index_ref, len_ref, seen_ref, weight_ref,
     out_ref, scale_ref, mask_ref, first_ref, slot_seen_ref, slot_weight_ref,
     swap_int, swap_float) = refs[far:]
    blocks, lags, cells = table_ref.shape
    slots, wide = out_ref.shape
    stations, hours = index_ref.shape
    per, part = hours // slots, GROUP * stations
    groups = blocks // GROUP
    core, shard = lax.axis_index("stn"), lax.axis_index("tm")
    pieces = {0: own_ref[...]}
    moved_refs = list(moved_refs)
    for group in grouped_fwd(far, 3):
        got = moved_refs.pop(0)[...]
        both = [got]
        if len(group) == 2:
            other = moved_refs.pop(0)[...]
            both = [jnp.where(core == i, got, other) for i in (0, 1)]
        for distance, piece in zip(group, both):
            pieces[distance] = jnp.where(shard >= distance, piece, jnp.zeros_like(piece))
    pieces = [pieces[d] for d in range(far + 1)]
    window = jnp.concatenate(pieces[::-1], 0)
    scale = lane_scale(block_scale_ref, groups)
    scale_ref[...] = scale
    mask = reach_mask(len_ref, lags, stations, per, wide)
    mask_ref[...] = mask
    lane = lax.broadcasted_iota(jnp.int32, (slots, wide), 1)
    rest = wide - per * part
    swap_int[...] = index_ref[...].T
    pieces = []
    for k in range(per):
        pieces += [swap_int[pl.ds(k, slots, stride=per), :]] * GROUP
    pieces += [jnp.zeros((slots, rest), jnp.int32)] if rest else []
    first = jnp.concatenate(pieces, axis=1) - lane % part // stations
    first_ref[...] = first
    for i, (source, target) in enumerate(((seen_ref, slot_seen_ref), (weight_ref, slot_weight_ref))):
        swap_float[i] = source[...].T
        pieces = []
        for k in range(per):
            pieces.append(swap_float[i, pl.ds(k, slots, stride=per), :])
            pieces.append(jnp.zeros((slots, part - stations), F32))
        pieces += [jnp.zeros((slots, rest), F32)] if rest else []
        target[...] = jnp.concatenate(pieces, axis=1)
    terms = []
    for g in range(groups):
        table = table_ref[g * GROUP : (g + 1) * GROUP].reshape(GROUP * lags, cells)
        if g < groups - 1:
            products = lax.dot_general(
                table, window, (((1,), (1,)), ((), ())), preferred_element_type=F32
            ).T
        else:
            products = lax.dot_general(
                window, table, (((1,), (1,)), ((), ())), preferred_element_type=F32
            )
        terms.append(skew_down(products, lags, slots) * scale[g : g + 1])
    early = two_term_dot(jnp.concatenate(terms[:-2], 0), mask, 0)
    late = two_term_dot(jnp.concatenate(terms[-2:], 0), mask, 0)
    sums = jnp.concatenate([early, late], 0)
    picked = jnp.zeros((slots, wide), F32)
    for g in range(groups):
        picked = jnp.where(first == g * GROUP, sums[g * slots : (g + 1) * slots], picked)
    total = picked
    for i in range(1, GROUP):
        total = total + pltpu.roll(picked, wide - i * stations, 1)
    out_ref[...] = total


def return_kernel(per, stations, *refs):
    (mine_ref, other_ref, seen_ref, weight_ref, flux_ref, prior_ref, table_ref, scale_ref,
     mask_ref, first_ref, resid_ref, own_ref, *rest) = refs
    *sent_refs, spread_ref = rest
    blocks, lags, cells = table_ref.shape
    slots, wide = mine_ref.shape
    part = GROUP * stations
    groups = blocks // GROUP
    rows = spread_ref.shape[0]
    shard = lax.axis_index("tm")
    scale = scale_ref[...]
    mask = mask_ref[...]
    first = first_ref[...]
    lane = lax.broadcasted_iota(jnp.int32, (slots, wide), 1)
    held = (lane % part < stations) & (lane < per * part)
    resid = jnp.where(held, weight_ref[...] * (mine_ref[...] + other_ref[...] - seen_ref[...]), 0.0)
    resid_ref[...] = resid
    spreading = resid
    for i in range(1, GROUP):
        spreading = spreading + pltpu.roll(resid, i * stations, 1)
    placed = [jnp.where(first == g * GROUP, spreading, 0.0) for g in range(groups)]
    lagged = two_term_dot(jnp.concatenate(placed, 0), mask, 1)
    for g in range(groups):
        term = lagged[g * slots : (g + 1) * slots] * scale[g : g + 1]
        spread = skew_up(term, lags, rows).astype(BF16)
        spread_ref[:, g * GROUP * lags : (g + 1) * GROUP * lags] = spread
    table = table_ref[...].reshape(blocks * lags, cells)
    returned = jnp.dot(spread_ref[...], table, preferred_element_type=F32)
    own_ref[...] = returned[rows - slots :] + 0.5 * prior_ref[...] * flux_ref[...]
    core = lax.axis_index("stn")
    near = []
    for distance in range(1, rows // slots):
        start = rows - slots * (distance + 1)
        piece = returned[start : start + slots]
        near.append(jnp.where(shard >= distance, piece, jnp.zeros_like(piece)))
    sent_refs = list(sent_refs)
    for group in grouped_fwd(len(near), 3):
        if len(group) == 1:
            sent = sent_refs.pop(0)
            sent[...] = near[group[0] - 1].astype(sent.dtype)
        else:
            first, second = near[group[0] - 1], near[group[1] - 1]
            sent_refs.pop(0)[...] = jnp.where(core == 1, first, second)
            sent_refs.pop(0)[...] = jnp.where(core == 0, first, second)


def order_kernel(slot_resid_ref, resid_ref, swap_float):
    stations, hours = resid_ref.shape
    slots, part = slot_resid_ref.shape[0], GROUP * stations
    per = hours // slots
    for k in range(per):
        swap_float[pl.ds(k, slots, stride=per), :] = slot_resid_ref[:, k * part : k * part + stations]
    resid_ref[...] = swap_float[...].T


PARAMS = pltpu.CompilerParams(vmem_limit_bytes=12 * 1024 * 1024)
VMEM = pl.BlockSpec(memory_space=pltpu.VMEM)


def on_device(
    fluxes, prior_weight, footprint, block_scale, block_index, foot_length, observed, obs_weight
):
    slots, cells = fluxes.shape
    blocks, lags, _ = footprint.shape
    hours, stations = block_index.shape
    far = min(lags // slots, lax.axis_size("tm") - 1)
    rows = slots * (far + 1)
    own = fluxes
    for flops in (10**4, 2 * 10**10):
        own = pl.pallas_call(
            round_kernel,
            out_shape=jax.ShapeDtypeStruct((slots, cells), BF16),
            in_specs=[VMEM],
            out_specs=VMEM,
            compiler_params=pltpu.CompilerParams(vmem_limit_bytes=2 * 1024 * 1024),
            cost_estimate=pl.CostEstimate(flops=flops, bytes_accessed=10**5, transcendentals=0),
        )(own)
    moved = []
    for group in grouped_fwd(far, 3):
        if len(group) == 1:
            moved.append(straight(own, group[0]))
        else:
            got = shared(own, group)
            moved += [got, swapped_sum(got, "stn")]
    per = hours // slots
    groups = blocks // GROUP
    wide = -(-per * GROUP * stations // 128) * 128
    by_hour = jax.ShapeDtypeStruct((slots, wide), F32)
    flops = 2 * blocks * lags * cells * rows
    nbytes = blocks * lags * cells * 2
    cost = pl.CostEstimate(flops=flops, bytes_accessed=nbytes, transcendentals=0)
    mine, scale, mask, first, seen, weight = pl.pallas_call(
        functools.partial(model_kernel, far),
        out_shape=[
            by_hour,
            jax.ShapeDtypeStruct((groups, GROUP * lags), F32),
            jax.ShapeDtypeStruct((GROUP * lags, wide), BF16),
            jax.ShapeDtypeStruct((slots, wide), jnp.int32),
            by_hour,
            by_hour,
        ],
        in_specs=[VMEM] * (far + 7),
        out_specs=[VMEM] * 6,
        scratch_shapes=[pltpu.VMEM((hours, stations), jnp.int32), pltpu.VMEM((2, hours, stations), F32)],
        compiler_params=PARAMS,
        cost_estimate=cost,
    )(*moved, own, footprint, block_scale, block_index.T, foot_length.reshape(1, stations), observed.T, obs_weight.T)
    other = swapped_sum(mine, "space")
    piece = jax.ShapeDtypeStruct((slots, cells), F32)
    sent = jax.ShapeDtypeStruct((slots, cells), BF16)
    resid, total, *back = pl.pallas_call(
        functools.partial(return_kernel, per, stations),
        out_shape=[by_hour, piece] + [piece] * (far // 2 * 2) + [sent] * (far % 2),
        in_specs=[VMEM] * 10,
        out_specs=[VMEM] * (2 + far),
        scratch_shapes=[pltpu.VMEM((rows, blocks * lags), BF16)],
        compiler_params=PARAMS,
        cost_estimate=cost,
    )(mine, other, seen, weight, fluxes, prior_weight, footprint, scale, mask, first)
    arrived = []
    for group in grouped_fwd(far, 3):
        if len(group) == 1:
            arrived.append(rolled(back.pop(0), -group[0]))
        else:
            both = back.pop(0) + swapped_sum(back.pop(0), "stn")
            arrived.append(shared(both.astype(BF16), [-d for d in group]))
    for piece in arrived[::-1]:
        total = total + piece
    resid = pl.pallas_call(
        order_kernel,
        out_shape=jax.ShapeDtypeStruct((stations, hours), F32),
        in_specs=[VMEM],
        out_specs=VMEM,
        scratch_shapes=[pltpu.VMEM((hours, stations), F32)],
        compiler_params=pltpu.CompilerParams(vmem_limit_bytes=2 * 1024 * 1024),
        cost_estimate=pl.CostEstimate(flops=10**6, bytes_accessed=10**4, transcendentals=0),
    )(resid)
    gradient = total + swapped_sum(total, "stn")
    return (resid.T, gradient)


def swapped_sum(x, axis):
    devices = lax.axis_size(axis)
    total = None
    for by in range(1, devices):
        moved = lax.ppermute(x, axis, [(i, (i + by) % devices) for i in range(devices)])
        total = moved if total is None else total + moved
    return jnp.zeros_like(x) if total is None else total


def solution(mesh):
    placed = (
        P("tm", ("parts", "space")),
        P("tm", ("parts", "space")),
        P(("tm", "stn"), None, ("parts", "space")),
        P(("parts", "tm", "stn"), None),
        P(("parts", "tm"), "stn"),
        P(("parts", "stn")),
        P(("parts", "tm"), "stn"),
        P(("parts", "tm"), "stn"),
    )
    return jax.shard_map(
        on_device,
        mesh=mesh,
        in_specs=placed,
        out_specs=(P(("parts", "tm"), "stn"), P("tm", ("parts", "space"))),
        check_vma=False,
    )
```

```python
import functools

import jax
import jax.numpy as jnp
from jax import lax
from jax.experimental import pallas as pl
from jax.experimental.pallas import tpu as pltpu
from jax.sharding import PartitionSpec as P

F32 = jnp.float32
BF16 = jnp.bfloat16
GROUP = 4


def rolled(x, by):
    devices = lax.axis_size("tm")
    pairs = [(t * 2 + c, (t + by) % devices * 2 + 1 - c) for t in range(devices) for c in (0, 1)]
    return lax.ppermute(x, ("tm", "stn"), pairs)


def straight(x, by):
    devices = lax.axis_size("tm")
    return lax.ppermute(x, "tm", [(t, (t + by) % devices) for t in range(devices)])


def grouped(far, single):
    rest = [d for d in range(1, far + 1) if d != single or far % 2 == 0]
    groups = [(rest[i + 1], rest[i]) for i in range(0, len(rest), 2)]
    return groups + [(single,)] * (far % 2)


def grouped_fwd(far, single):
    return [g[::-1] for g in grouped(far, single)]


def shared(x, by):
    devices = lax.axis_size("tm")
    pairs = [
        (t * 2 + 1 - core, (t + by[core]) % devices * 2 + core)
        for t in range(devices)
        for core in (0, 1)
    ]
    return lax.ppermute(x, ("tm", "stn"), pairs)


def reach_mask(len_ref, lags, stations, per, wide):
    shape = (GROUP * lags, wide)
    lengths = jnp.concatenate([len_ref[...]] * (wide // stations), axis=1)
    row = lax.broadcasted_iota(jnp.int32, shape, 0)
    col = lax.broadcasted_iota(jnp.int32, shape, 1)
    part = GROUP * stations
    same = ((row // lags) == (col % part // stations)) & (col < per * part)
    return jnp.where(same & ((row % lags) < lengths), 1.0, 0.0).astype(BF16)


def lane_scale(scale_ref, groups):
    return jnp.concatenate(
        [scale_ref[pl.ds(i, groups, stride=GROUP), :] for i in range(GROUP)], axis=1
    )


def lag_bits(lags, rows):
    lag = lax.broadcasted_iota(jnp.int32, (rows, GROUP * lags), 1) % lags
    return lag


def two_term_dot(x, mask, contract):
    high = x.astype(BF16)
    low = (x - high.astype(F32)).astype(BF16)
    dims = (((1,), (contract,)), ((), ()))
    return lax.dot_general(high, mask, dims, preferred_element_type=F32) + lax.dot_general(
        low, mask, dims, preferred_element_type=F32
    )


def skew_down(x, lags, slots):
    need = slots + lags
    rows = x.shape[0]
    if rows < need:
        x = jnp.concatenate([jnp.zeros((need - rows, x.shape[1]), x.dtype), x], 0)
    step = lags // 2
    while step >= 8:
        keep = x.shape[0] - step
        bit = (lag_bits(lags, keep) & step) != 0
        x = jnp.where(bit, x[:keep], x[step:])
        step //= 2
    while step >= 1:
        bit = (lag_bits(lags, x.shape[0]) & step) != 0
        x = jnp.where(bit, pltpu.roll(x, step, 0), x)
        step //= 2
    return x[x.shape[0] - slots :]


def skew_up(x, lags, rows):
    slots, lanes = x.shape
    x = jnp.concatenate([jnp.zeros((8, lanes), x.dtype), x], 0)
    step = 1
    while step < 8:
        bit = (lag_bits(lags, x.shape[0]) & step) != 0
        x = jnp.where(bit, pltpu.roll(x, x.shape[0] - step, 0), x)
        step *= 2
    while step < lags:
        gap = jnp.zeros((step, lanes), x.dtype)
        bit = (lag_bits(lags, x.shape[0] + step) & step) != 0
        x = jnp.where(bit, jnp.concatenate([x, gap], 0), jnp.concatenate([gap, x], 0))
        step *= 2
    return x[x.shape[0] - rows :]


def fetch_kernel(flux_hbm, out_ref, flux_ref, sems):
    part = flux_ref.shape[1] // 4
    at = [(slice(None), pl.ds(i * part, part)) for i in range(4)]
    copies = [
        pltpu.make_async_copy(flux_hbm.at[at[i]], flux_ref.at[at[i]], sems.at[i]) for i in range(4)
    ]
    for copy in copies:
        copy.start()
    for i, copy in enumerate(copies):
        copy.wait()
        out_ref[at[i]] = flux_ref[at[i]].astype(out_ref.dtype)


def pass_kernel(in_ref, out_ref):
    out_ref[...] = in_ref[...]


def model_kernel(far, *refs):
    moved_refs = refs[: far]
    (own_ref, table_ref, block_scale_ref, index_ref, len_ref, seen_ref, weight_ref,
     out_ref, scale_ref, mask_ref, first_ref, slot_seen_ref, slot_weight_ref,
     swap_int, swap_float) = refs[far:]
    blocks, lags, cells = table_ref.shape
    slots, wide = out_ref.shape
    stations, hours = index_ref.shape
    per, part = hours // slots, GROUP * stations
    groups = blocks // GROUP
    core, shard = lax.axis_index("stn"), lax.axis_index("tm")
    pieces = {0: own_ref[...]}
    moved_refs = list(moved_refs)
    for group in grouped_fwd(far, 3):
        got = moved_refs.pop(0)[...]
        both = [got]
        if len(group) == 2:
            other = moved_refs.pop(0)[...]
            both = [jnp.where(core == i, got, other) for i in (0, 1)]
        for distance, piece in zip(group, both):
            pieces[distance] = jnp.where(shard >= distance, piece, jnp.zeros_like(piece))
    pieces = [pieces[d] for d in range(far + 1)]
    window = jnp.concatenate(pieces[::-1], 0)
    scale = lane_scale(block_scale_ref, groups)
    scale_ref[...] = scale
    mask = reach_mask(len_ref, lags, stations, per, wide)
    mask_ref[...] = mask
    lane = lax.broadcasted_iota(jnp.int32, (slots, wide), 1)
    rest = wide - per * part
    swap_int[...] = index_ref[...].T
    pieces = []
    for k in range(per):
        pieces += [swap_int[pl.ds(k, slots, stride=per), :]] * GROUP
    pieces += [jnp.zeros((slots, rest), jnp.int32)] if rest else []
    first = jnp.concatenate(pieces, axis=1) - lane % part // stations
    first_ref[...] = first
    for i, (source, target) in enumerate(((seen_ref, slot_seen_ref), (weight_ref, slot_weight_ref))):
        swap_float[i] = source[...].T
        pieces = []
        for k in range(per):
            pieces.append(swap_float[i, pl.ds(k, slots, stride=per), :])
            pieces.append(jnp.zeros((slots, part - stations), F32))
        pieces += [jnp.zeros((slots, rest), F32)] if rest else []
        target[...] = jnp.concatenate(pieces, axis=1)
    terms = []
    for g in range(groups):
        table = table_ref[g * GROUP : (g + 1) * GROUP].reshape(GROUP * lags, cells)
        if g < groups - 3:
            products = lax.dot_general(
                table, window, (((1,), (1,)), ((), ())), preferred_element_type=F32
            ).T
        else:
            products = lax.dot_general(
                window, table, (((1,), (1,)), ((), ())), preferred_element_type=F32
            )
        terms.append(skew_down(products, lags, slots) * scale[g : g + 1])
    early = two_term_dot(jnp.concatenate(terms[:-4], 0), mask, 0)
    late = two_term_dot(jnp.concatenate(terms[-4:], 0), mask, 0)
    sums = jnp.concatenate([early, late], 0)
    picked = jnp.zeros((slots, wide), F32)
    for g in range(groups):
        picked = jnp.where(first == g * GROUP, sums[g * slots : (g + 1) * slots], picked)
    total = picked
    for i in range(1, GROUP):
        total = total + pltpu.roll(picked, wide - i * stations, 1)
    out_ref[...] = total


def return_kernel(per, stations, *refs):
    (mine_ref, other_ref, seen_ref, weight_ref, flux_ref, prior_ref, table_ref, scale_ref,
     mask_ref, first_ref, resid_ref, own_ref, *rest) = refs
    *sent_refs, spread_ref = rest
    blocks, lags, cells = table_ref.shape
    slots, wide = mine_ref.shape
    part = GROUP * stations
    groups = blocks // GROUP
    rows = spread_ref.shape[0]
    shard = lax.axis_index("tm")
    scale = scale_ref[...]
    mask = mask_ref[...]
    first = first_ref[...]
    lane = lax.broadcasted_iota(jnp.int32, (slots, wide), 1)
    held = (lane % part < stations) & (lane < per * part)
    resid = jnp.where(held, weight_ref[...] * (mine_ref[...] + other_ref[...] - seen_ref[...]), 0.0)
    resid_ref[...] = resid
    spreading = resid
    for i in range(1, GROUP):
        spreading = spreading + pltpu.roll(resid, i * stations, 1)
    placed = [jnp.where(first == g * GROUP, spreading, 0.0) for g in range(groups)]
    lagged = two_term_dot(jnp.concatenate(placed, 0), mask, 1)
    for g in range(groups):
        term = lagged[g * slots : (g + 1) * slots] * scale[g : g + 1]
        spread = skew_up(term, lags, rows).astype(BF16)
        spread_ref[:, g * GROUP * lags : (g + 1) * GROUP * lags] = spread
    table = table_ref[...].reshape(blocks * lags, cells)
    returned = jnp.dot(spread_ref[...], table, preferred_element_type=F32)
    own_ref[...] = returned[rows - slots :] + 0.5 * prior_ref[...] * flux_ref[...]
    core = lax.axis_index("stn")
    near = []
    for distance in range(1, rows // slots):
        start = rows - slots * (distance + 1)
        piece = returned[start : start + slots]
        near.append(jnp.where(shard >= distance, piece, jnp.zeros_like(piece)))
    sent_refs = list(sent_refs)
    for group in grouped_fwd(len(near), 3):
        if len(group) == 1:
            sent = sent_refs.pop(0)
            sent[...] = near[group[0] - 1].astype(sent.dtype)
        else:
            first, second = near[group[0] - 1], near[group[1] - 1]
            sent_refs.pop(0)[...] = jnp.where(core == 1, first, second)
            sent_refs.pop(0)[...] = jnp.where(core == 0, first, second)


def order_kernel(slot_resid_ref, resid_ref, swap_float):
    stations, hours = resid_ref.shape
    slots, part = slot_resid_ref.shape[0], GROUP * stations
    per = hours // slots
    for k in range(per):
        swap_float[pl.ds(k, slots, stride=per), :] = slot_resid_ref[:, k * part : k * part + stations]
    resid_ref[...] = swap_float[...].T


PARAMS = pltpu.CompilerParams(vmem_limit_bytes=12 * 1024 * 1024)
VMEM = pl.BlockSpec(memory_space=pltpu.VMEM)


def on_device(
    fluxes, prior_weight, footprint, block_scale, block_index, foot_length, observed, obs_weight
):
    slots, cells = fluxes.shape
    blocks, lags, _ = footprint.shape
    hours, stations = block_index.shape
    far = min(lags // slots, lax.axis_size("tm") - 1)
    rows = slots * (far + 1)
    half = jax.ShapeDtypeStruct((slots, cells), BF16)
    small = pltpu.CompilerParams(vmem_limit_bytes=2 * 1024 * 1024)
    own = pl.pallas_call(
        fetch_kernel,
        out_shape=half,
        in_specs=[pl.BlockSpec(memory_space=pltpu.HBM)],
        out_specs=VMEM,
        scratch_shapes=[pltpu.VMEM((slots, cells), F32), pltpu.SemaphoreType.DMA((4,))],
        compiler_params=small,
        cost_estimate=pl.CostEstimate(flops=10**4, bytes_accessed=10**5, transcendentals=0),
    )(pltpu.with_memory_space_constraint(fluxes, pltpu.HBM))
    own = pl.pallas_call(
        pass_kernel,
        out_shape=half,
        in_specs=[VMEM],
        out_specs=VMEM,
        compiler_params=small,
        cost_estimate=pl.CostEstimate(flops=2 * 10**10, bytes_accessed=10**5, transcendentals=0),
    )(own)
    moved = []
    for group in grouped_fwd(far, 3):
        if len(group) == 1:
            moved.append(straight(own, group[0]))
        else:
            got = shared(own, group)
            moved += [got, swapped_sum(got, "stn")]
    per = hours // slots
    groups = blocks // GROUP
    wide = -(-per * GROUP * stations // 128) * 128
    by_hour = jax.ShapeDtypeStruct((slots, wide), F32)
    flops = 2 * blocks * lags * cells * rows
    nbytes = blocks * lags * cells * 2
    cost = pl.CostEstimate(flops=flops, bytes_accessed=nbytes, transcendentals=0)
    mine, scale, mask, first, seen, weight = pl.pallas_call(
        functools.partial(model_kernel, far),
        out_shape=[
            by_hour,
            jax.ShapeDtypeStruct((groups, GROUP * lags), F32),
            jax.ShapeDtypeStruct((GROUP * lags, wide), BF16),
            jax.ShapeDtypeStruct((slots, wide), jnp.int32),
            by_hour,
            by_hour,
        ],
        in_specs=[VMEM] * (far + 7),
        out_specs=[VMEM] * 6,
        scratch_shapes=[pltpu.VMEM((hours, stations), jnp.int32), pltpu.VMEM((2, hours, stations), F32)],
        compiler_params=PARAMS,
        cost_estimate=cost,
    )(*moved, own, footprint, block_scale, block_index.T, foot_length.reshape(1, stations), observed.T, obs_weight.T)
    other = swapped_sum(mine, "space")
    piece = jax.ShapeDtypeStruct((slots, cells), F32)
    sent = jax.ShapeDtypeStruct((slots, cells), BF16)
    resid, total, *back = pl.pallas_call(
        functools.partial(return_kernel, per, stations),
        out_shape=[by_hour, piece] + [piece] * (far // 2 * 2) + [sent] * (far % 2),
        in_specs=[VMEM] * 10,
        out_specs=[VMEM] * (2 + far),
        scratch_shapes=[pltpu.VMEM((rows, blocks * lags), BF16)],
        compiler_params=PARAMS,
        cost_estimate=cost,
    )(mine, other, seen, weight, fluxes, prior_weight, footprint, scale, mask, first)
    arrived = []
    for group in grouped_fwd(far, 3):
        if len(group) == 1:
            arrived.append(rolled(back.pop(0), -group[0]))
        else:
            both = back.pop(0) + swapped_sum(back.pop(0), "stn")
            arrived.append(shared(both.astype(BF16), [-d for d in group]))
    for piece in arrived[::-1]:
        total = total + piece
    resid = pl.pallas_call(
        order_kernel,
        out_shape=jax.ShapeDtypeStruct((stations, hours), F32),
        in_specs=[VMEM],
        out_specs=VMEM,
        scratch_shapes=[pltpu.VMEM((hours, stations), F32)],
        compiler_params=pltpu.CompilerParams(vmem_limit_bytes=2 * 1024 * 1024),
        cost_estimate=pl.CostEstimate(flops=10**6, bytes_accessed=10**4, transcendentals=0),
    )(resid)
    gradient = total + swapped_sum(total, "stn")
    return (resid.T, gradient)


def swapped_sum(x, axis):
    devices = lax.axis_size(axis)
    total = None
    for by in range(1, devices):
        moved = lax.ppermute(x, axis, [(i, (i + by) % devices) for i in range(devices)])
        total = moved if total is None else total + moved
    return jnp.zeros_like(x) if total is None else total


def solution(mesh):
    placed = (
        P("tm", ("parts", "space")),
        P("tm", ("parts", "space")),
        P(("tm", "stn"), None, ("parts", "space")),
        P(("parts", "tm", "stn"), None),
        P(("parts", "tm"), "stn"),
        P(("parts", "stn")),
        P(("parts", "tm"), "stn"),
        P(("parts", "tm"), "stn"),
    )
    return jax.shard_map(
        on_device,
        mesh=mesh,
        in_specs=placed,
        out_specs=(P(("parts", "tm"), "stn"), P("tm", ("parts", "space"))),
        check_vma=False,
    )
```

```python
import functools

import jax
import jax.numpy as jnp
from jax import lax
from jax.experimental import pallas as pl
from jax.experimental.pallas import tpu as pltpu
from jax.sharding import PartitionSpec as P

F32 = jnp.float32
BF16 = jnp.bfloat16
GROUP = 4


def rolled(x, by):
    devices = lax.axis_size("tm")
    pairs = [(t * 2 + c, (t + by) % devices * 2 + 1 - c) for t in range(devices) for c in (0, 1)]
    return lax.ppermute(x, ("tm", "stn"), pairs)


def straight(x, by):
    devices = lax.axis_size("tm")
    return lax.ppermute(x, "tm", [(t, (t + by) % devices) for t in range(devices)])


def grouped(far, single):
    rest = [d for d in range(1, far + 1) if d != single or far % 2 == 0]
    groups = [(rest[i + 1], rest[i]) for i in range(0, len(rest), 2)]
    return groups + [(single,)] * (far % 2)


def grouped_fwd(far, single):
    return [g[::-1] for g in grouped(far, single)]


def shared(x, by):
    devices = lax.axis_size("tm")
    pairs = [
        (t * 2 + 1 - core, (t + by[core]) % devices * 2 + core)
        for t in range(devices)
        for core in (0, 1)
    ]
    return lax.ppermute(x, ("tm", "stn"), pairs)


def reach_mask(len_ref, lags, stations, per, wide):
    shape = (GROUP * lags, wide)
    lengths = jnp.concatenate([len_ref[...]] * (wide // stations), axis=1)
    row = lax.broadcasted_iota(jnp.int32, shape, 0)
    col = lax.broadcasted_iota(jnp.int32, shape, 1)
    part = GROUP * stations
    same = ((row // lags) == (col % part // stations)) & (col < per * part)
    return jnp.where(same & ((row % lags) < lengths), 1.0, 0.0).astype(BF16)


def lane_scale(scale_ref, groups):
    return jnp.concatenate(
        [scale_ref[pl.ds(i, groups, stride=GROUP), :] for i in range(GROUP)], axis=1
    )


def lag_bits(lags, rows):
    lag = lax.broadcasted_iota(jnp.int32, (rows, GROUP * lags), 1) % lags
    return lag


def two_term_dot(x, mask, contract):
    high = x.astype(BF16)
    low = (x - high.astype(F32)).astype(BF16)
    dims = (((1,), (contract,)), ((), ()))
    return lax.dot_general(high, mask, dims, preferred_element_type=F32) + lax.dot_general(
        low, mask, dims, preferred_element_type=F32
    )


def skew_down(x, lags, slots):
    need = slots + lags
    rows = x.shape[0]
    if rows < need:
        x = jnp.concatenate([jnp.zeros((need - rows, x.shape[1]), x.dtype), x], 0)
    step = lags // 2
    while step >= 8:
        keep = x.shape[0] - step
        bit = (lag_bits(lags, keep) & step) != 0
        x = jnp.where(bit, x[:keep], x[step:])
        step //= 2
    while step >= 1:
        bit = (lag_bits(lags, x.shape[0]) & step) != 0
        x = jnp.where(bit, pltpu.roll(x, step, 0), x)
        step //= 2
    return x[x.shape[0] - slots :]


def skew_up(x, lags, rows):
    slots, lanes = x.shape
    x = jnp.concatenate([jnp.zeros((8, lanes), x.dtype), x], 0)
    step = 1
    while step < 8:
        bit = (lag_bits(lags, x.shape[0]) & step) != 0
        x = jnp.where(bit, pltpu.roll(x, x.shape[0] - step, 0), x)
        step *= 2
    while step < lags:
        gap = jnp.zeros((step, lanes), x.dtype)
        bit = (lag_bits(lags, x.shape[0] + step) & step) != 0
        x = jnp.where(bit, jnp.concatenate([x, gap], 0), jnp.concatenate([gap, x], 0))
        step *= 2
    return x[x.shape[0] - rows :]


def fetch_kernel(flux_hbm, out_ref, flux_ref, sems):
    part = flux_ref.shape[1] // 4
    at = [(slice(None), pl.ds(i * part, part)) for i in range(4)]
    copies = [
        pltpu.make_async_copy(flux_hbm.at[at[i]], flux_ref.at[at[i]], sems.at[i]) for i in range(4)
    ]
    for copy in copies:
        copy.start()
    for i, copy in enumerate(copies):
        copy.wait()
        out_ref[at[i]] = flux_ref[at[i]].astype(out_ref.dtype)


def pass_kernel(in_ref, out_ref):
    out_ref[...] = in_ref[...]


def model_kernel(far, *refs):
    moved_refs = refs[: far]
    (own_ref, table_ref, block_scale_ref, index_ref, len_ref, seen_ref, weight_ref,
     out_ref, scale_ref, mask_ref, first_ref, slot_seen_ref, slot_weight_ref,
     swap_int, swap_float) = refs[far:]
    blocks, lags, cells = table_ref.shape
    slots, wide = out_ref.shape
    stations, hours = index_ref.shape
    per, part = hours // slots, GROUP * stations
    groups = blocks // GROUP
    core, shard = lax.axis_index("stn"), lax.axis_index("tm")
    pieces = {0: own_ref[...]}
    moved_refs = list(moved_refs)
    for group in grouped_fwd(far, 3):
        got = moved_refs.pop(0)[...]
        both = [got]
        if len(group) == 2:
            other = moved_refs.pop(0)[...]
            both = [jnp.where(core == i, got, other) for i in (0, 1)]
        for distance, piece in zip(group, both):
            pieces[distance] = jnp.where(shard >= distance, piece, jnp.zeros_like(piece))
    pieces = [pieces[d] for d in range(far + 1)]
    window = jnp.concatenate(pieces[::-1], 0)
    scale = lane_scale(block_scale_ref, groups)
    scale_ref[...] = scale
    mask = reach_mask(len_ref, lags, stations, per, wide)
    mask_ref[...] = mask
    lane = lax.broadcasted_iota(jnp.int32, (slots, wide), 1)
    rest = wide - per * part
    swap_int[...] = index_ref[...].T
    pieces = []
    for k in range(per):
        pieces += [swap_int[pl.ds(k, slots, stride=per), :]] * GROUP
    pieces += [jnp.zeros((slots, rest), jnp.int32)] if rest else []
    first = jnp.concatenate(pieces, axis=1) - lane % part // stations
    first_ref[...] = first
    for i, (source, target) in enumerate(((seen_ref, slot_seen_ref), (weight_ref, slot_weight_ref))):
        swap_float[i] = source[...].T
        pieces = []
        for k in range(per):
            pieces.append(swap_float[i, pl.ds(k, slots, stride=per), :])
            pieces.append(jnp.zeros((slots, part - stations), F32))
        pieces += [jnp.zeros((slots, rest), F32)] if rest else []
        target[...] = jnp.concatenate(pieces, axis=1)
    terms = []
    for g in range(groups):
        table = table_ref[g * GROUP : (g + 1) * GROUP].reshape(GROUP * lags, cells)
        if g < groups - 3:
            products = lax.dot_general(
                table, window, (((1,), (1,)), ((), ())), preferred_element_type=F32
            ).T
        else:
            products = lax.dot_general(
                window, table, (((1,), (1,)), ((), ())), preferred_element_type=F32
            )
        terms.append(skew_down(products, lags, slots) * scale[g : g + 1])
    early = two_term_dot(jnp.concatenate(terms[:-4], 0), mask, 0)
    late = two_term_dot(jnp.concatenate(terms[-4:], 0), mask, 0)
    sums = jnp.concatenate([early, late], 0)
    picked = jnp.zeros((slots, wide), F32)
    for g in range(groups):
        picked = jnp.where(first == g * GROUP, sums[g * slots : (g + 1) * slots], picked)
    total = picked
    for i in range(1, GROUP):
        total = total + pltpu.roll(picked, wide - i * stations, 1)
    out_ref[...] = total


def return_kernel(per, stations, *refs):
    (mine_ref, other_ref, seen_ref, weight_ref, table_ref, scale_ref,
     mask_ref, first_ref, resid_ref, own_ref, *rest) = refs
    *sent_refs, spread_ref = rest
    blocks, lags, cells = table_ref.shape
    slots, wide = mine_ref.shape
    part = GROUP * stations
    groups = blocks // GROUP
    rows = spread_ref.shape[0]
    shard = lax.axis_index("tm")
    scale = scale_ref[...]
    mask = mask_ref[...]
    first = first_ref[...]
    lane = lax.broadcasted_iota(jnp.int32, (slots, wide), 1)
    held = (lane % part < stations) & (lane < per * part)
    resid = jnp.where(held, weight_ref[...] * (mine_ref[...] + other_ref[...] - seen_ref[...]), 0.0)
    resid_ref[...] = resid
    spreading = resid
    for i in range(1, GROUP):
        spreading = spreading + pltpu.roll(resid, i * stations, 1)
    placed = [jnp.where(first == g * GROUP, spreading, 0.0) for g in range(groups)]
    lagged = two_term_dot(jnp.concatenate(placed, 0), mask, 1)
    for g in range(groups):
        term = lagged[g * slots : (g + 1) * slots] * scale[g : g + 1]
        spread = skew_up(term, lags, rows).astype(BF16)
        spread_ref[:, g * GROUP * lags : (g + 1) * GROUP * lags] = spread
    table = table_ref[...].reshape(blocks * lags, cells)
    returned = jnp.dot(spread_ref[...], table, preferred_element_type=F32)
    own_ref[...] = returned[rows - slots :]
    core = lax.axis_index("stn")
    near = []
    for distance in range(1, rows // slots):
        start = rows - slots * (distance + 1)
        piece = returned[start : start + slots]
        near.append(jnp.where(shard >= distance, piece, jnp.zeros_like(piece)))
    sent_refs = list(sent_refs)
    for group in grouped_fwd(len(near), 3):
        if len(group) == 1:
            sent = sent_refs.pop(0)
            sent[...] = near[group[0] - 1].astype(sent.dtype)
        else:
            first, second = near[group[0] - 1], near[group[1] - 1]
            sent_refs.pop(0)[...] = jnp.where(core == 1, first, second)
            sent_refs.pop(0)[...] = jnp.where(core == 0, first, second)


def order_kernel(slot_resid_ref, resid_ref, swap_float):
    stations, hours = resid_ref.shape
    slots, part = slot_resid_ref.shape[0], GROUP * stations
    per = hours // slots
    for k in range(per):
        swap_float[pl.ds(k, slots, stride=per), :] = slot_resid_ref[:, k * part : k * part + stations]
    resid_ref[...] = swap_float[...].T


PARAMS = pltpu.CompilerParams(vmem_limit_bytes=12 * 1024 * 1024)
VMEM = pl.BlockSpec(memory_space=pltpu.VMEM)


def on_device(
    fluxes, prior_weight, footprint, block_scale, block_index, foot_length, observed, obs_weight
):
    slots, cells = fluxes.shape
    blocks, lags, _ = footprint.shape
    hours, stations = block_index.shape
    far = min(lags // slots, lax.axis_size("tm") - 1)
    rows = slots * (far + 1)
    half = jax.ShapeDtypeStruct((slots, cells), BF16)
    small = pltpu.CompilerParams(vmem_limit_bytes=2 * 1024 * 1024)
    own = pl.pallas_call(
        fetch_kernel,
        out_shape=half,
        in_specs=[pl.BlockSpec(memory_space=pltpu.HBM)],
        out_specs=VMEM,
        scratch_shapes=[pltpu.VMEM((slots, cells), F32), pltpu.SemaphoreType.DMA((4,))],
        compiler_params=small,
        cost_estimate=pl.CostEstimate(flops=10**4, bytes_accessed=10**5, transcendentals=0),
    )(pltpu.with_memory_space_constraint(fluxes, pltpu.HBM))
    own = pl.pallas_call(
        pass_kernel,
        out_shape=half,
        in_specs=[VMEM],
        out_specs=VMEM,
        compiler_params=small,
        cost_estimate=pl.CostEstimate(flops=2 * 10**10, bytes_accessed=10**5, transcendentals=0),
    )(own)
    moved = []
    for group in grouped_fwd(far, 3):
        if len(group) == 1:
            moved.append(straight(own, group[0]))
        else:
            got = shared(own, group)
            moved += [got, swapped_sum(got, "stn")]
    per = hours // slots
    groups = blocks // GROUP
    wide = -(-per * GROUP * stations // 128) * 128
    by_hour = jax.ShapeDtypeStruct((slots, wide), F32)
    flops = 2 * blocks * lags * cells * rows
    nbytes = blocks * lags * cells * 2
    cost = pl.CostEstimate(flops=flops, bytes_accessed=nbytes, transcendentals=0)
    mine, scale, mask, first, seen, weight = pl.pallas_call(
        functools.partial(model_kernel, far),
        out_shape=[
            by_hour,
            jax.ShapeDtypeStruct((groups, GROUP * lags), F32),
            jax.ShapeDtypeStruct((GROUP * lags, wide), BF16),
            jax.ShapeDtypeStruct((slots, wide), jnp.int32),
            by_hour,
            by_hour,
        ],
        in_specs=[VMEM] * (far + 7),
        out_specs=[VMEM] * 6,
        scratch_shapes=[pltpu.VMEM((hours, stations), jnp.int32), pltpu.VMEM((2, hours, stations), F32)],
        compiler_params=PARAMS,
        cost_estimate=cost,
    )(*moved, own, footprint, block_scale, block_index.T, foot_length.reshape(1, stations), observed.T, obs_weight.T)
    other = swapped_sum(mine, "space")
    piece = jax.ShapeDtypeStruct((slots, cells), F32)
    sent = jax.ShapeDtypeStruct((slots, cells), BF16)
    resid, total, *back = pl.pallas_call(
        functools.partial(return_kernel, per, stations),
        out_shape=[by_hour, piece] + [piece] * (far // 2 * 2) + [sent] * (far % 2),
        in_specs=[VMEM] * 8,
        out_specs=[VMEM] * (2 + far),
        scratch_shapes=[pltpu.VMEM((rows, blocks * lags), BF16)],
        compiler_params=PARAMS,
        cost_estimate=cost,
    )(mine, other, seen, weight, footprint, scale, mask, first)
    arrived = []
    for group in grouped_fwd(far, 3):
        if len(group) == 1:
            arrived.append(rolled(back.pop(0), -group[0]))
        else:
            both = back.pop(0) + swapped_sum(back.pop(0), "stn")
            arrived.append(shared(both.astype(BF16), [-d for d in group]))
    total = total + 0.5 * prior_weight * fluxes
    for piece in arrived[::-1]:
        total = total + piece
    resid = pl.pallas_call(
        order_kernel,
        out_shape=jax.ShapeDtypeStruct((stations, hours), F32),
        in_specs=[VMEM],
        out_specs=VMEM,
        scratch_shapes=[pltpu.VMEM((hours, stations), F32)],
        compiler_params=pltpu.CompilerParams(vmem_limit_bytes=2 * 1024 * 1024),
        cost_estimate=pl.CostEstimate(flops=10**6, bytes_accessed=10**4, transcendentals=0),
    )(resid)
    gradient = total + swapped_sum(total, "stn")
    return (resid.T, gradient)


def swapped_sum(x, axis):
    devices = lax.axis_size(axis)
    total = None
    for by in range(1, devices):
        moved = lax.ppermute(x, axis, [(i, (i + by) % devices) for i in range(devices)])
        total = moved if total is None else total + moved
    return jnp.zeros_like(x) if total is None else total


def solution(mesh):
    placed = (
        P("tm", ("parts", "space")),
        P("tm", ("parts", "space")),
        P(("tm", "stn"), None, ("parts", "space")),
        P(("parts", "tm", "stn"), None),
        P(("parts", "tm"), "stn"),
        P(("parts", "stn")),
        P(("parts", "tm"), "stn"),
        P(("parts", "tm"), "stn"),
    )
    return jax.shard_map(
        on_device,
        mesh=mesh,
        in_specs=placed,
        out_specs=(P(("parts", "tm"), "stn"), P("tm", ("parts", "space"))),
        check_vma=False,
    )
```
